256 devices in a mesh: tm: 32 (over y, x, core), tile: 8 (over z).
Axes of the slice: x: 4, y: 4, z: 8, core: 2. Of those that a mesh axis runs over, the one named last changes fastest.
Arguments:
- input_frames: bfloat16 [256, 128, 256, 128], P('tm', 'tile'), may hold values from -24 to 24
- clip_spans: int32 [16], replicated, may hold values from 1 to 8, 64 in all
- conv_weight: bfloat16 [3, 3, 3, 128, 128], replicated, may hold values from -0.109375 to 0.109375
- norm_gain: float32 [128], replicated, may hold values from 0.5 to 1.5
- norm_bias: float32 [128], replicated, may hold values from -0.5 to 0.5
Outputs:
- output_frames: bfloat16 [128, 64, 128, 128], P('tm', 'tile')
The draws below stay inside these ranges and needn't reach their ends.
All inputs are finite; a program needn't handle non-finite values.
Results may differ from the reference program's by a relative error of at most 0.001.
Values may be sent and summed in bfloat16 or wider, within the bound.
A program may use at most 128 MiB of HBM per device.

```python
import math
import jax
import jax.numpy as jnp
import numpy as np
from jax import lax

C = 128
G = 32
F = 4
CH_DEV = 2
MOST_SPANS = 8
SLOTS = 64
CLIPS = 16
FRAMES = 256
HEIGHT = 128
WIDTH = 256
N_TM = 32


def draw_input_frames(key, part):
    key = jax.random.fold_in(key, 11)
    noise_key, frame_key = jax.random.split(key, 2)
    full_shape = (FRAMES, HEIGHT, WIDTH, C)
    row_index = jnp.arange(HEIGHT, dtype=jnp.float32)
    row_scale = 1.0 + 2.0 * row_index / (HEIGHT - 1)
    frame_scale = jnp.exp(jax.random.uniform(frame_key, (FRAMES,), jnp.float32, -0.7, 0.7))
    scales = frame_scale[:, None, None, None] * row_scale[None, :, None, None]
    values = jnp.clip(jax.random.normal(noise_key, full_shape, jnp.float32), -4.0, 4.0) * scales
    return jnp.clip(values, -24.0, 24.0).astype(jnp.bfloat16)


def length_profile(count, total, most, slope):
    loads = [(1 << 20) // math.isqrt(grade ** slope) + 1 for grade in range(2, count + 1)]
    spare, holding = total - most - (count - 1), [1] * (count - 1)
    while spare > 0:
        free = [i for i in range(count - 1) if holding[i] < most]
        pool, budget = sum([loads[i] for i in free]), spare
        for i in free:
            more = min(most - holding[i], max(1, budget * loads[i] // pool), spare)
            holding[i] = holding[i] + more
            spare = spare - more
    return np.array([most] + holding)


def ragged_sizes(stream_key, number_of, total, most, skew):
    if number_of == 2:
        one = jax.random.randint(stream_key, (), max(1, total - most), min(most, total - 1) + 1)
        return jnp.stack([one, total - one])
    sizes = jnp.asarray(length_profile(number_of, total, most, skew), jnp.int32)
    twos = (number_of - 1) // 2
    source_of, sink = sizes[1:1 + 2 * twos:2], sizes[2:2 + 2 * twos:2]
    slack = jnp.minimum(source_of - 1, most - sink)
    moved = jax.random.randint(jax.random.fold_in(stream_key, 1), (twos,), 0, 1 << 20) % (slack + 1)
    sizes = sizes.at[1:1 + 2 * twos:2].set(source_of - moved).at[2:2 + 2 * twos:2].set(sink + moved)
    return sizes[jax.random.permutation(jax.random.fold_in(stream_key, 2), number_of)]


def normal_values(own_key, extent, scale, bound, kind=jnp.bfloat16):
    entries = scale * jax.random.normal(own_key, extent, jnp.float32)
    return jnp.clip(entries, min=-bound, max=bound).astype(kind)


def setup_inputs(seed: int = 0) -> dict:
    arg_keys = jax.random.split(jax.random.key(seed), 6)
    return {
        "input_frames": draw_input_frames(jax.random.fold_in(arg_keys[5], 71), 0),
        "clip_spans": ragged_sizes(arg_keys[1], CLIPS, SLOTS, MOST_SPANS, 2).astype(jnp.int32),
        "conv_weight": normal_values(arg_keys[2], (3, 3, 3, C, C), (27 * C) ** -0.5, 0.109375),
        "norm_gain": jnp.clip(jax.random.uniform(arg_keys[3], (C,), jnp.float32, 0.5, 1.5), 0.5, 1.5),
        "norm_bias": jnp.clip(jax.random.uniform(arg_keys[4], (C,), jnp.float32, -0.5, 0.5), -0.5, 0.5),
    }


def reference(input_frames, clip_spans, conv_weight, norm_gain, norm_bias):
    slots = CH_DEV * N_TM
    frames_all, height, width_in, channels = input_frames.shape
    blocks = input_frames.reshape(slots, F, height, width_in, channels)
    clip_ends = jnp.cumsum(clip_spans)
    starts = clip_ends - clip_spans
    slot_ids = jnp.arange(slots, dtype=jnp.int32)
    slot_clip = lax.optimization_barrier(jnp.sum((slot_ids[:, None] >= clip_ends[None, :]).astype(jnp.int32), axis=1))
    is_start = jnp.any(slot_ids[:, None] == starts[None, :], axis=1)
    kernel = conv_weight.astype(jnp.float32)

    def one_slot(index):
        block = blocks[index]
        prior = blocks[jnp.maximum(index - 1, 0).astype(jnp.int32)][F - 2:]
        first_pair = jnp.stack([block[0], block[0]])
        prior_pair = jnp.where(is_start[index], first_pair, prior)
        extended = jnp.concatenate([prior_pair, block], axis=0).astype(jnp.float32)
        result = lax.conv_general_dilated(extended[None], kernel, (2, 2, 2), [(0, 0), (1, 0), (1, 0)], dimension_numbers=('NDHWC', 'DHWIO', 'NDHWC'), precision=lax.Precision.HIGHEST)
        return result[0]
    conv_out = lax.map(one_slot, slot_ids)
    group_size = channels // G
    slot_to_clip = (slot_clip[:, None] == jnp.arange(CLIPS, dtype=jnp.int32)[None, :]).astype(jnp.float32)
    grouping = (jnp.arange(channels, dtype=jnp.int32)[:, None] // group_size == jnp.arange(G, dtype=jnp.int32)[None, :]).astype(jnp.float32)
    counts = clip_spans.astype(jnp.float32) * (F // 2 * (height // 2) * (width_in // 2) * group_size)
    high = lax.Precision.HIGHEST

    def to_groups(per_slot):
        return jnp.dot(jnp.dot(slot_to_clip.T, per_slot, precision=high), grouping, precision=high)

    def to_channels(per_clip):
        return jnp.dot(jnp.dot(slot_to_clip, per_clip, precision=high), grouping.T, precision=high)
    means = to_groups(lax.optimization_barrier(jnp.sum(conv_out, axis=(1, 2, 3)))) / counts[:, None]
    centered = conv_out - to_channels(means)[:, None, None, None, :]
    variance = to_groups(lax.optimization_barrier(jnp.sum(centered * centered, axis=(1, 2, 3)))) / counts[:, None]
    inverse = to_channels(lax.rsqrt(variance + 1e-06))
    normed = centered * inverse[:, None, None, None, :] * norm_gain + norm_bias
    output = jax.nn.silu(normed).astype(jnp.bfloat16)
    return output.reshape(slots * (F // 2), height // 2, width_in // 2, channels)
```

```python
import functools

import jax
import jax.numpy as jnp
from jax import lax
from jax.experimental import pallas as pl
from jax.experimental.pallas import tpu as pltpu
from jax.sharding import PartitionSpec as P

F = 4
CH_DEV = 2
GROUP = 4
REACH = 4
EPS = 1e-6
MESH = pl.DeviceIdType.MESH
f32, bf16 = jnp.float32, jnp.bfloat16


def kernel(
    n_tm, n_tile, rows, cols, chans,
    spans, x_hbm, w_hbm, y_hbm, stat_out,
    xb, xe, xo, wt, y, p_send, c_send, p_recv, c_recv, z_send, z_recv,
    mine, from_tile, pooled, from_tm,
    in_sem, w_sem, out_sem, ps_sem, pr_sem, cs_sem, cr_sem, zs_sem, zr_sem,
    as_sem, ar_sem, bs_sem, br_sem,
):
    tm, tile = lax.axis_index("tm"), lax.axis_index("tile")
    half, c2 = rows // 2, 2 * chans
    m_rows = half * cols
    reach = [k for k in range(-REACH, REACH + 1) if k]

    def at_tm(k):
        return {"tm": lax.rem(tm + k + n_tm, n_tm)}

    def at_tile(k):
        return {"tile": lax.rem(tile + k, n_tile)}

    def remote(src, dst, send, recv, where):
        return pltpu.make_async_remote_copy(
            src_ref=src, dst_ref=dst, send_sem=send, recv_sem=recv, device_id=where, device_id_type=MESH
        )

    order = (6, 7, 0, 4, 5, 2, 3, 1)
    loads = {f: pltpu.make_async_copy(x_hbm.at[f], xb.at[f], in_sem.at[f]) for f in order}
    w_loads = [
        pltpu.make_async_copy(w_hbm.at[:, 1], wt.at[:, 0:chans, 0:chans], w_sem.at[0]),
        pltpu.make_async_copy(w_hbm.at[:, 2], wt.at[:, chans:c2, 0:chans], w_sem.at[1]),
        pltpu.make_async_copy(w_hbm.at[:, 0], wt.at[:, chans:c2, chans:c2], w_sem.at[2]),
    ]
    loads[6].start()
    for copy in w_loads:
        copy.start()
    for f in order[1:]:
        loads[f].start()

    barrier = pltpu.get_barrier_semaphore()
    for k in range(1, n_tile):
        pl.semaphore_signal(barrier, inc=1, device_id=at_tile(k), device_id_type=MESH)
    for k in reach:
        pl.semaphore_signal(barrier, inc=1, device_id=at_tm(k), device_id_type=MESH)

    ends, total = [], jnp.int32(0)
    for c in range(spans.shape[0]):
        total = total + spans[c]
        ends.append(total)
    lows, highs = [], []
    for m in range(CH_DEV):
        slot = tm * CH_DEV + m
        lo, hi = jnp.int32(0), jnp.int32(n_tm * CH_DEV)
        for end in ends:
            lo = jnp.maximum(lo, jnp.where(end <= slot, end, 0))
            hi = jnp.minimum(hi, jnp.where(end > slot, end, n_tm * CH_DEV))
        lows.append(lo)
        highs.append(hi)
    opens = [(lows[m] == tm * CH_DEV + m) for m in range(CH_DEV)]

    wt[:, 0:chans, chans:c2] = jnp.zeros((wt.shape[0], chans, chans), bf16)
    for f in range(xo.shape[0]):
        xo[f, 0] = jnp.zeros((cols, c2), bf16)

    def pair_columns(raw, f):
        for r in range(rows):
            pair = raw(r).reshape(cols, c2)
            if r % 2:
                xo[f, 1 + r // 2] = pair
            else:
                xe[f, r // 2] = pair

    def joined(both):
        moved = pltpu.roll(both[:, chans:c2], 1, 0)
        column = lax.broadcasted_iota(jnp.int32, moved.shape, 0) % cols
        return both[:, 0:chans] + jnp.where(column == 0, 0.0, moved)

    def taps(pairs, first=0, count=None):
        count = half if count is None else count
        sums = None
        for a, f in pairs:
            for b, part in ((0, xo[f, first : first + count]), (1, xe[f, first : first + count]),
                            (2, xo[f, first + 1 : first + 1 + count])):
                one = jnp.dot(part.reshape(count * cols, c2), wt[3 * a + b], preferred_element_type=f32)
                sums = one if sums is None else sums + one
        return joined(sums)

    def below(pairs):
        sums = None
        for a, f in pairs:
            one = jnp.dot(xo[f, half], wt[3 * a], preferred_element_type=f32)
            sums = one if sums is None else sums + one
        return joined(sums)

    def ready(f):
        loads[f].wait()
        pair_columns(lambda r: xb[f, r], f)

    ready(6)
    ready(7)
    for copy in w_loads:
        copy.wait()

    passed = ((0, 6), (1, 7))
    c_send[...] = below(passed)
    quarter = half // 2
    p_send[0] = taps(passed, 0, quarter)
    pl.semaphore_wait(barrier, n_tile - 1 + len(reach))
    corner = remote(c_send, c_recv, cs_sem, cr_sem, at_tm(1))
    corner.start()
    partial = [remote(p_send.at[i], p_recv.at[i], ps_sem.at[i], pr_sem.at[i], at_tm(1)) for i in range(2)]
    partial[0].start()
    p_send[1] = taps(passed, quarter, quarter)
    partial[1].start()

    edge = [remote(z_send.at[k], z_recv.at[k], zs_sem.at[k], zr_sem.at[k], at_tile(1)) for k in range(4)]

    ready(0)
    y[0] = taps(((2, 0),))
    own = taps(((0, 0), (1, 0)))
    p_own = own
    z_first = below(((2, 0),))
    z_own = below(((0, 0), (1, 0)))

    ready(4)
    ready(5)
    z_send[3] = below(((0, 4), (1, 5), (2, 6)))
    edge[3].start()
    y[3] = taps(((0, 4), (1, 5), (2, 6)))

    corner.wait_recv()
    z_send[0] = z_first + jnp.where(opens[0], z_own, c_recv[...])
    edge[0].start()

    ready(2)
    loads[3].wait()
    pair_columns(lambda r: jnp.where(opens[1], xb[4, r], xb[3, r]), 3)
    pair_columns(lambda r: jnp.where(opens[1], xb[4, r], xb[2, r]), 8)
    z_send[2] = below(((0, 8), (1, 3), (2, 4)))
    edge[2].start()
    y[2] = taps(((0, 8), (1, 3), (2, 4)))

    ready(1)
    z_send[1] = below(((0, 0), (1, 1), (2, 2)))
    edge[1].start()
    y[1] = taps(((0, 0), (1, 1), (2, 2)))

    stores = [pltpu.make_async_copy(y.at[k], y_hbm.at[k], out_sem.at[k]) for k in range(4)]

    def finish(k):
        edge[k].wait_recv()
        y[k, 0:cols] = y[k, 0:cols] + jnp.where(tile == 0, 0.0, z_recv[k])
        if k == 0:
            for i in range(2):
                partial[i].wait_recv()
                part = pl.ds(i * quarter * cols, quarter * cols)
                y[k, part] = y[k, part] + jnp.where(opens[0], p_own[i * quarter * cols : (i + 1) * quarter * cols], p_recv[i])
        stores[k].start()
        mean = jnp.sum(y[k], axis=0, keepdims=True) * (1.0 / m_rows)
        off = y[k] - mean
        return mean, jnp.sum(off * off, axis=0, keepdims=True)

    def pool(means, squares, count):
        mean = functools.reduce(jnp.add, means) * (1.0 / len(means))
        apart = functools.reduce(jnp.add, [(m - mean) * (m - mean) for m in means])
        return mean, functools.reduce(jnp.add, squares) + count * apart

    part = [None] * 4
    for k in (3, 2, 1, 0):
        part[k] = finish(k)
    count = m_rows
    blocks = [pool([part[2 * m][0], part[2 * m + 1][0]], [part[2 * m][1], part[2 * m + 1][1]], count) for m in range(CH_DEV)]
    count *= 2

    fill = jnp.zeros((8 - 2 * CH_DEV, chans), f32)

    def packed(stats):
        return jnp.concatenate([s[0] for s in stats] + [s[1] for s in stats] + [fill], axis=0)

    mine[...] = packed(blocks)
    to_tiles = [
        remote(mine, from_tile.at[k - 1], as_sem.at[k - 1], ar_sem.at[k - 1], at_tile(k)) for k in range(1, n_tile)
    ]
    for copy in to_tiles:
        copy.start()
    for copy in to_tiles:
        copy.wait_recv()
    all_means = [mine[0:CH_DEV]] + [from_tile[k, 0:CH_DEV] for k in range(n_tile - 1)]
    all_squares = [mine[CH_DEV : 2 * CH_DEV]] + [from_tile[k, CH_DEV : 2 * CH_DEV] for k in range(n_tile - 1)]
    mean, square = pool(all_means, all_squares, count)
    count *= n_tile
    pooled[...] = jnp.concatenate([mean, square, fill], axis=0)

    to_tm = [remote(pooled, from_tm.at[i], bs_sem.at[i], br_sem.at[i], at_tm(k)) for i, k in enumerate(reach)]
    for copy in to_tm:
        copy.start()
    for copy in to_tm:
        copy.wait_recv()
    held = [(tm, pooled[...])] + [(tm - k, from_tm[i]) for i, k in enumerate(reach)]

    lane = lax.broadcasted_iota(jnp.int32, (1, chans), 1)

    def over_group(v):
        step = 1
        while step < GROUP:
            v = v + jnp.where((lane // step) % 2 == 1, pltpu.roll(v, step, 1), pltpu.roll(v, chans - step, 1))
            step *= 2
        return v

    rows_out = []
    for m in range(CH_DEV):
        shares = []
        for device, stats in held:
            for q in range(CH_DEV):
                slot = device * CH_DEV + q
                inside = jnp.logical_and(slot >= lows[m], slot < highs[m])
                shares.append((inside, stats[q : q + 1], stats[CH_DEV + q : CH_DEV + q + 1]))
        spans_here = jnp.full((1, chans), (highs[m] - lows[m]).astype(f32))
        clip_mean = functools.reduce(jnp.add, [jnp.where(i, a, 0.0) for i, a, _ in shares]) / spans_here
        mean = over_group(clip_mean) * (1.0 / GROUP)
        spread = functools.reduce(
            jnp.add, [jnp.where(i, s + count * ((a - mean) * (a - mean)), 0.0) for i, a, s in shares]
        )
        variance = over_group(spread) / (spans_here * float(count * GROUP))
        rows_out += [mean, lax.rsqrt(variance + EPS)]
    stat_out[...] = jnp.concatenate(rows_out + [fill], axis=0)

    for copy in stores:
        copy.wait()
    corner.wait_send()
    for copy in partial + edge + to_tiles + to_tm:
        copy.wait_send()


def body(input_frames, clip_spans, conv_weight, norm_gain, norm_bias):
    frames, rows, width, chans = input_frames.shape
    n_tm, n_tile = lax.axis_size("tm"), lax.axis_size("tile")
    half, cols = rows // 2, width // 2
    m_rows = half * cols
    weights = conv_weight.reshape(9, 3, chans, chans)
    n_reach = 2 * REACH
    dma = pltpu.SemaphoreType.DMA
    hbm, vmem = pl.BlockSpec(memory_space=pl.ANY), pl.BlockSpec(memory_space=pltpu.VMEM)
    y, stats = pl.pallas_call(
        functools.partial(kernel, n_tm, n_tile, rows, cols, chans),
        out_shape=[jax.ShapeDtypeStruct((4, m_rows, chans), f32), jax.ShapeDtypeStruct((8, chans), f32)],
        in_specs=[pl.BlockSpec(memory_space=pltpu.SMEM), hbm, hbm],
        out_specs=[hbm, vmem],
        scratch_shapes=[
            pltpu.VMEM((frames, rows, width, chans), bf16),
            pltpu.VMEM((frames + 1, half, cols, 2 * chans), bf16),
            pltpu.VMEM((frames + 1, half + 1, cols, 2 * chans), bf16),
            pltpu.VMEM((9, 2 * chans, 2 * chans), bf16),
            pltpu.VMEM((4, m_rows, chans), f32),
            pltpu.VMEM((2, m_rows // 2, chans), f32),
            pltpu.VMEM((cols, chans), f32),
            pltpu.VMEM((2, m_rows // 2, chans), f32),
            pltpu.VMEM((cols, chans), f32),
            pltpu.VMEM((4, cols, chans), f32),
            pltpu.VMEM((4, cols, chans), f32),
            pltpu.VMEM((8, chans), f32),
            pltpu.VMEM((n_tile - 1, 8, chans), f32),
            pltpu.VMEM((8, chans), f32),
            pltpu.VMEM((n_reach, 8, chans), f32),
            dma((frames,)), dma((3,)), dma((4,)),
            dma((2,)), dma((2,)), dma, dma, dma((4,)), dma((4,)),
            dma((n_tile - 1,)), dma((n_tile - 1,)), dma((n_reach,)), dma((n_reach,)),
        ],
        compiler_params=pltpu.CompilerParams(
            collective_id=0, has_side_effects=True, vmem_limit_bytes=56 * 2**20
        ),
    )(clip_spans, input_frames, weights)
    y = y.reshape(CH_DEV, F // 2, half, cols, chans)
    mean, inverse = stats[0:4:2].reshape(2, 1, 1, 1, chans), stats[1:4:2].reshape(2, 1, 1, 1, chans)
    normed = (y - mean) * inverse * norm_gain + norm_bias
    return jax.nn.silu(normed).astype(bf16).reshape(CH_DEV * (F // 2), half, cols, chans)


def solution(mesh):
    in_specs = (P("tm", "tile", None, None), P(), P(), P(), P())
    out_specs = P("tm", "tile", None, None)
    return jax.shard_map(body, mesh=mesh, in_specs=in_specs, out_specs=out_specs, check_vma=False)
```

```python
import functools

import jax
import jax.numpy as jnp
from jax import lax
from jax.experimental import pallas as pl
from jax.experimental.pallas import tpu as pltpu
from jax.sharding import PartitionSpec as P

F = 4
CH_DEV = 2
GROUP = 4
REACH = 4
EPS = 1e-6
MESH = pl.DeviceIdType.MESH
f32, bf16 = jnp.float32, jnp.bfloat16


def kernel(
    n_tm, n_tile, rows, cols, chans,
    spans_hbm, x_hbm, w_hbm, y, stat_out,
    spans, xb, xe, xo, wt, p_own, p_send, c_send, p_recv, c_recv, z_send, z_recv,
    mine, from_tile, pooled, from_tm,
    spans_sem, in_sem, w_sem, ps_sem, pr_sem, cs_sem, cr_sem, zs_sem, zr_sem,
    as_sem, ar_sem, bs_sem, br_sem,
):
    tm, tile = lax.axis_index("tm"), lax.axis_index("tile")
    half, c2 = rows // 2, 2 * chans
    m_rows = half * cols
    reach = [k for k in range(-REACH, REACH + 1) if k]

    def at_tm(k):
        return {"tm": lax.rem(tm + k + n_tm, n_tm)}

    def at_tile(k):
        return {"tile": lax.rem(tile + k, n_tile)}

    def remote(src, dst, send, recv, where):
        return pltpu.make_async_remote_copy(
            src_ref=src, dst_ref=dst, send_sem=send, recv_sem=recv, device_id=where, device_id_type=MESH
        )

    order = (6, 7, 0, 4, 5, 2, 3, 1)
    loads = {f: pltpu.make_async_copy(x_hbm.at[f], xb.at[f], in_sem.at[f]) for f in order}
    w_loads = [
        pltpu.make_async_copy(w_hbm.at[:, 1], wt.at[:, 0:chans, 0:chans], w_sem.at[0]),
        pltpu.make_async_copy(w_hbm.at[:, 2], wt.at[:, chans:c2, 0:chans], w_sem.at[1]),
        pltpu.make_async_copy(w_hbm.at[:, 0], wt.at[:, chans:c2, chans:c2], w_sem.at[2]),
    ]
    spans_load = pltpu.make_async_copy(spans_hbm, spans, spans_sem)
    spans_load.start()
    loads[6].start()
    for copy in w_loads:
        copy.start()
    for f in order[1:]:
        loads[f].start()

    barrier = pltpu.get_barrier_semaphore()
    for k in range(1, n_tile):
        pl.semaphore_signal(barrier, inc=1, device_id=at_tile(k), device_id_type=MESH)
    for k in reach:
        pl.semaphore_signal(barrier, inc=1, device_id=at_tm(k), device_id_type=MESH)

    spans_load.wait()
    ends, total = [], jnp.int32(0)
    for c in range(spans.shape[0]):
        total = total + spans[c]
        ends.append(total)
    lows, highs = [], []
    for m in range(CH_DEV):
        slot = tm * CH_DEV + m
        lo, hi = jnp.int32(0), jnp.int32(n_tm * CH_DEV)
        for end in ends:
            lo = jnp.maximum(lo, jnp.where(end <= slot, end, 0))
            hi = jnp.minimum(hi, jnp.where(end > slot, end, n_tm * CH_DEV))
        lows.append(lo)
        highs.append(hi)
    opens = [(lows[m] == tm * CH_DEV + m) for m in range(CH_DEV)]

    wt[:, 0:chans, chans:c2] = jnp.zeros((wt.shape[0], chans, chans), bf16)
    for f in range(xo.shape[0]):
        xo[f, 0] = jnp.zeros((cols, c2), bf16)

    def pair_columns(raw, f):
        for r in range(rows):
            pair = raw(r).reshape(cols, c2)
            if r % 2:
                xo[f, 1 + r // 2] = pair
            else:
                xe[f, r // 2] = pair

    def joined(both):
        moved = pltpu.roll(both[:, chans:c2], 1, 0)
        column = lax.broadcasted_iota(jnp.int32, moved.shape, 0) % cols
        return both[:, 0:chans] + jnp.where(column == 0, 0.0, moved)

    def taps(pairs, into):
        step = half // 2
        for part in range(2):
            first = part * step
            sums = None
            for a, f in pairs:
                for b, lhs in ((0, xo[f, first : first + step]), (1, xe[f, first : first + step]),
                               (2, xo[f, first + 1 : first + 1 + step])):
                    one = jnp.dot(lhs.reshape(step * cols, c2), wt[3 * a + b], preferred_element_type=f32)
                    sums = one if sums is None else sums + one
            into[first * cols : (first + step) * cols] = joined(sums)

    def below(pairs):
        sums = None
        for a, f in pairs:
            one = jnp.dot(xo[f, half], wt[3 * a], preferred_element_type=f32)
            sums = one if sums is None else sums + one
        return joined(sums)

    def ready(f):
        loads[f].wait()
        pair_columns(lambda r: xb[f, r], f)

    ready(6)
    ready(7)
    for copy in w_loads:
        copy.wait()

    passed = ((0, 6), (1, 7))
    size = m_rows // 2
    c_send[...] = below(passed)
    taps(passed, p_send)
    pl.semaphore_wait(barrier, n_tile - 1 + len(reach))
    corner = remote(c_send, c_recv, cs_sem, cr_sem, at_tm(1))
    corner.start()
    partial = [
        remote(p_send.at[pl.ds(i * size, size)], p_recv.at[pl.ds(i * size, size)], ps_sem.at[i], pr_sem.at[i], at_tm(1))
        for i in range(2)
    ]
    for copy in partial:
        copy.start()

    edge = [remote(z_send.at[k], z_recv.at[k], zs_sem.at[k], zr_sem.at[k], at_tile(1)) for k in range(4)]

    ready(0)
    ready(4)
    ready(5)
    z_send[3] = below(((0, 4), (1, 5), (2, 6)))
    z_first = below(((2, 0),))
    z_own = below(((0, 0), (1, 0)))
    taps(((2, 0),), y.at[0])
    taps(((0, 0), (1, 0)), p_own)
    taps(((0, 4), (1, 5), (2, 6)), y.at[3])
    edge[3].start()

    corner.wait_recv()
    z_send[0] = z_first + jnp.where(opens[0], z_own, c_recv[...])
    edge[0].start()

    ready(2)
    loads[3].wait()
    pair_columns(lambda r: jnp.where(opens[1], xb[4, r], xb[3, r]), 3)
    pair_columns(lambda r: jnp.where(opens[1], xb[4, r], xb[2, r]), 8)
    ready(1)
    z_send[2] = below(((0, 8), (1, 3), (2, 4)))
    z_send[1] = below(((0, 0), (1, 1), (2, 2)))
    edge[2].start()
    edge[1].start()
    taps(((0, 8), (1, 3), (2, 4)), y.at[2])
    taps(((0, 0), (1, 1), (2, 2)), y.at[1])

    def finish(k):
        edge[k].wait_recv()
        y[k, 0:cols] = y[k, 0:cols] + jnp.where(tile == 0, 0.0, z_recv[k])
        if k == 0:
            for copy in partial:
                copy.wait_recv()
            y[k] = y[k] + jnp.where(opens[0], p_own[...], p_recv[...])
        mean = jnp.sum(y[k], axis=0, keepdims=True) * (1.0 / m_rows)
        off = y[k] - mean
        return mean, jnp.sum(off * off, axis=0, keepdims=True)

    def pool(means, squares, count):
        mean = functools.reduce(jnp.add, means) * (1.0 / len(means))
        apart = functools.reduce(jnp.add, [(m - mean) * (m - mean) for m in means])
        return mean, functools.reduce(jnp.add, squares) + count * apart

    part = [None] * 4
    for k in (3, 2, 1, 0):
        part[k] = finish(k)
    count = m_rows
    blocks = [pool([part[2 * m][0], part[2 * m + 1][0]], [part[2 * m][1], part[2 * m + 1][1]], count) for m in range(CH_DEV)]
    count *= 2

    fill = jnp.zeros((8 - 2 * CH_DEV, chans), f32)

    def packed(stats):
        return jnp.concatenate([s[0] for s in stats] + [s[1] for s in stats] + [fill], axis=0)

    mine[...] = packed(blocks)
    to_tiles = [
        remote(mine, from_tile.at[k - 1], as_sem.at[k - 1], ar_sem.at[k - 1], at_tile(k)) for k in range(1, n_tile)
    ]
    for copy in to_tiles:
        copy.start()
    for copy in to_tiles:
        copy.wait_recv()
    all_means = [mine[0:CH_DEV]] + [from_tile[k, 0:CH_DEV] for k in range(n_tile - 1)]
    all_squares = [mine[CH_DEV : 2 * CH_DEV]] + [from_tile[k, CH_DEV : 2 * CH_DEV] for k in range(n_tile - 1)]
    mean, square = pool(all_means, all_squares, count)
    count *= n_tile
    pooled[...] = jnp.concatenate([mean, square, fill], axis=0)

    to_tm = [remote(pooled, from_tm.at[i], bs_sem.at[i], br_sem.at[i], at_tm(k)) for i, k in enumerate(reach)]
    for copy in to_tm:
        copy.start()
    for copy in to_tm:
        copy.wait_recv()
    held = [(tm, pooled[...])] + [(tm - k, from_tm[i]) for i, k in enumerate(reach)]

    lane = lax.broadcasted_iota(jnp.int32, (1, chans), 1)

    def over_group(v):
        step = 1
        while step < GROUP:
            v = v + jnp.where((lane // step) % 2 == 1, pltpu.roll(v, step, 1), pltpu.roll(v, chans - step, 1))
            step *= 2
        return v

    rows_out = []
    for m in range(CH_DEV):
        shares = []
        for device, stats in held:
            for q in range(CH_DEV):
                slot = device * CH_DEV + q
                inside = jnp.logical_and(slot >= lows[m], slot < highs[m])
                shares.append((inside, stats[q : q + 1], stats[CH_DEV + q : CH_DEV + q + 1]))
        spans_here = jnp.full((1, chans), (highs[m] - lows[m]).astype(f32))
        clip_mean = functools.reduce(jnp.add, [jnp.where(i, a, 0.0) for i, a, _ in shares]) / spans_here
        mean = over_group(clip_mean) * (1.0 / GROUP)
        spread = functools.reduce(
            jnp.add, [jnp.where(i, s + count * ((a - mean) * (a - mean)), 0.0) for i, a, s in shares]
        )
        variance = over_group(spread) / (spans_here * float(count * GROUP))
        rows_out += [mean, lax.rsqrt(variance + EPS)]
    stat_out[...] = jnp.concatenate(rows_out + [fill], axis=0)

    corner.wait_send()
    for copy in partial + edge + to_tiles + to_tm:
        copy.wait_send()


def finishing(y, stats, gain, bias, out_hbm, out, sem):
    copies = []
    for k in range(y.shape[0]):
        m = k // (F // 2)
        normed = (y[k] - stats[2 * m : 2 * m + 1]) * stats[2 * m + 1 : 2 * m + 2] * gain[...] + bias[...]
        halved = 0.5 * normed
        out[k] = (halved * jnp.tanh(halved) + halved).astype(bf16)
        copies.append(pltpu.make_async_copy(out.at[k], out_hbm.at[k], sem.at[k]))
        copies[-1].start()
    for copy in copies:
        copy.wait()


def body(input_frames, clip_spans, conv_weight, norm_gain, norm_bias):
    frames, rows, width, chans = input_frames.shape
    n_tm, n_tile = lax.axis_size("tm"), lax.axis_size("tile")
    half, cols = rows // 2, width // 2
    m_rows = half * cols
    outs = CH_DEV * (F // 2)
    weights = conv_weight.reshape(9, 3, chans, chans)
    n_reach = 2 * REACH
    dma = pltpu.SemaphoreType.DMA
    any_space, vmem = pl.BlockSpec(memory_space=pl.ANY), pl.BlockSpec(memory_space=pltpu.VMEM)
    y, stats = pl.pallas_call(
        functools.partial(kernel, n_tm, n_tile, rows, cols, chans),
        out_shape=[pltpu.VMEM((outs, m_rows, chans), f32), pltpu.VMEM((8, chans), f32)],
        in_specs=[any_space] * 3,
        out_specs=[vmem, vmem],
        scratch_shapes=[
            pltpu.SMEM(clip_spans.shape, jnp.int32),
            pltpu.VMEM((frames, rows, width, chans), bf16),
            pltpu.VMEM((frames + 1, half, cols, 2 * chans), bf16),
            pltpu.VMEM((frames + 1, half + 1, cols, 2 * chans), bf16),
            pltpu.VMEM((9, 2 * chans, 2 * chans), bf16),
            pltpu.VMEM((m_rows, chans), f32),
            pltpu.VMEM((m_rows, chans), f32),
            pltpu.VMEM((cols, chans), f32),
            pltpu.VMEM((m_rows, chans), f32),
            pltpu.VMEM((cols, chans), f32),
            pltpu.VMEM((outs, cols, chans), f32),
            pltpu.VMEM((outs, cols, chans), f32),
            pltpu.VMEM((8, chans), f32),
            pltpu.VMEM((n_tile - 1, 8, chans), f32),
            pltpu.VMEM((8, chans), f32),
            pltpu.VMEM((n_reach, 8, chans), f32),
            dma, dma((frames,)), dma((3,)),
            dma((2,)), dma((2,)), dma, dma, dma((4,)), dma((4,)),
            dma((n_tile - 1,)), dma((n_tile - 1,)), dma((n_reach,)), dma((n_reach,)),
        ],
        compiler_params=pltpu.CompilerParams(
            collective_id=0, has_side_effects=True, vmem_limit_bytes=48 * 2**20
        ),
    )(
        pltpu.with_memory_space_constraint(clip_spans, pltpu.HBM),
        input_frames,
        pltpu.with_memory_space_constraint(weights, pltpu.HBM),
    )
    out = pl.pallas_call(
        finishing,
        out_shape=jax.ShapeDtypeStruct((outs, m_rows, chans), bf16),
        in_specs=[vmem] * 4,
        out_specs=any_space,
        scratch_shapes=[pltpu.VMEM((outs, m_rows, chans), bf16), dma((outs,))],
        compiler_params=pltpu.CompilerParams(vmem_limit_bytes=16 * 2**20),
    )(
        pltpu.with_memory_space_constraint(y, pltpu.VMEM),
        pltpu.with_memory_space_constraint(stats, pltpu.VMEM),
        norm_gain.reshape(1, chans),
        norm_bias.reshape(1, chans),
    )
    return out.reshape(outs, half, cols, chans)


def solution(mesh):
    in_specs = (P("tm", "tile", None, None), P(), P(), P(), P())
    out_specs = P("tm", "tile", None, None)
    return jax.shard_map(body, mesh=mesh, in_specs=in_specs, out_specs=out_specs, check_vma=False)
```

```python
import functools

import jax
import jax.numpy as jnp
from jax import lax
from jax.experimental import pallas as pl
from jax.experimental.pallas import tpu as pltpu
from jax.sharding import PartitionSpec as P

F = 4
CH_DEV = 2
GROUP = 4
REACH = 4
EPS = 1e-6
CODES = 32767.0
TINY = 1e-30
MESH = pl.DeviceIdType.MESH
f32, bf16 = jnp.float32, jnp.bfloat16


def kernel(
    n_tm, n_tile, rows, cols, chans,
    spans_hbm, x_hbm, w_hbm, y, stat_out,
    spans, rb, ro, xb, xe, xo, wt, p_own, p_raw, p_send, p_most, c_send, c_most, z_send, z_most,
    p_recv, p_scale, c_recv, c_scale, z_recv, z_scale,
    mine, from_tile, pooled, from_tm,
    spans_sem, row_sem, in_sem, w_sem, halo_send, halo_recv, as_sem, ar_sem, bs_sem, br_sem,
):
    tm, tile = lax.axis_index("tm"), lax.axis_index("tile")
    half, c2 = rows // 2, 2 * chans
    m_rows = half * cols
    reach = [sign * k for k in range(REACH, 0, -1) for sign in (-1, 1)]
    around = sorted(range(1, n_tile), key=lambda k: -min(k, n_tile - k))

    def at_tm(k):
        return {"tm": lax.rem(tm + k + n_tm, n_tm)}

    def at_tile(k):
        return {"tile": lax.rem(tile + k, n_tile)}

    def aslant(k):
        return {"tm": lax.rem(tm + k + n_tm, n_tm), "tile": lax.rem(tile + k + n_tile, n_tile)}

    def remote(src, dst, send, recv, where):
        return pltpu.make_async_remote_copy(
            src_ref=src, dst_ref=dst, send_sem=send, recv_sem=recv, device_id=where, device_id_type=MESH
        )

    order = (6, 7, 0, 4, 5, 2, 3, 1)
    loads = {f: pltpu.make_async_copy(x_hbm.at[f], xb.at[f], in_sem.at[f]) for f in order}
    w_loads = []
    for a in range(3):
        from_w, to_w = w_hbm.at[3 * a : 3 * a + 3], wt.at[3 * a : 3 * a + 3]
        w_loads.append([
            pltpu.make_async_copy(from_w.at[:, 1], to_w.at[:, 0:chans, 0:chans], w_sem.at[a, 0]),
            pltpu.make_async_copy(from_w.at[:, 2], to_w.at[:, chans:c2, 0:chans], w_sem.at[a, 1]),
            pltpu.make_async_copy(from_w.at[:, 0], to_w.at[:, chans:c2, chans:c2], w_sem.at[a, 2]),
        ])
    spans_load = pltpu.make_async_copy(spans_hbm, spans, spans_sem)
    row_load = pltpu.make_async_copy(x_hbm.at[:, rows - 1], rb, row_sem)
    row_load.start()
    for a in range(3):
        for copy in w_loads[a]:
            copy.start()
    spans_load.start()
    for f in order:
        loads[f].start()

    barrier = pltpu.get_barrier_semaphore()
    for k in range(1, n_tile):
        pl.semaphore_signal(barrier, inc=1, device_id=at_tile(k), device_id_type=MESH)
    for k in reach:
        pl.semaphore_signal(barrier, inc=1, device_id=at_tm(k), device_id_type=MESH)
    for k in (-1, 1):
        pl.semaphore_signal(barrier, inc=1, device_id=aslant(k), device_id_type=MESH)

    spans_load.wait()
    ends, total = [], jnp.int32(0)
    for c in range(spans.shape[0]):
        total = total + spans[c]
        ends.append(total)
    lows, highs = [], []
    for m in range(CH_DEV):
        slot = tm * CH_DEV + m
        lo, hi = jnp.int32(0), jnp.int32(n_tm * CH_DEV)
        for end in ends:
            lo = jnp.maximum(lo, jnp.where(end <= slot, end, 0))
            hi = jnp.minimum(hi, jnp.where(end > slot, end, n_tm * CH_DEV))
        lows.append(lo)
        highs.append(hi)
    opens = [(lows[m] == tm * CH_DEV + m) for m in range(CH_DEV)]

    wt[:, 0:chans, chans:c2] = jnp.zeros((wt.shape[0], chans, chans), bf16)
    for f in range(xo.shape[0]):
        xo[f, 0] = jnp.zeros((cols, c2), bf16)

    def pair_columns(raw, f):
        for r in range(rows):
            pair = raw(r).reshape(cols, c2)
            if r % 2:
                xo[f, 1 + r // 2] = pair
            else:
                xe[f, r // 2] = pair

    def joined(both):
        moved = pltpu.roll(both[:, chans:c2], 1, 0)
        column = lax.broadcasted_iota(jnp.int32, moved.shape, 0) % cols
        return both[:, 0:chans] + jnp.where(column == 0, 0.0, moved)

    def taps(pairs, into, add=False):
        step = half // 2
        for part in range(2):
            first = part * step
            sums = None
            for a, f in pairs:
                for b, lhs in ((0, xo[f, first : first + step]), (1, xe[f, first : first + step]),
                               (2, xo[f, first + 1 : first + 1 + step])):
                    one = jnp.dot(lhs.reshape(step * cols, c2), wt[3 * a + b], preferred_element_type=f32)
                    sums = one if sums is None else sums + one
            there = slice(first * cols, (first + step) * cols)
            into[there] = into[there] + joined(sums) if add else joined(sums)

    def encode(value, codes, there, most, r):
        top = jnp.maximum(jnp.max(jnp.abs(value), axis=0, keepdims=True), TINY)
        most[r : r + 1] = top
        codes[there] = jnp.round(value * (CODES / top)).astype(jnp.int32).astype(jnp.int16)

    def decode(codes, there, most, r):
        return codes[there].astype(jnp.int32).astype(f32) * (most[r : r + 1] * (1.0 / CODES))

    def row_of(r):
        return slice(r * cols, (r + 1) * cols)

    def ready(f):
        loads[f].wait()
        pair_columns(lambda r: xb[f, r], f)

    def w_ready(a):
        for copy in w_loads[a]:
            copy.wait()

    row_load.wait()
    for f in range(xb.shape[0]):
        ro[f] = rb[f].reshape(cols, c2)
    earlier = [jnp.where(opens[1], ro[4], ro[f]) for f in (2, 3)]
    for a in range(3):
        for copy in w_loads[a]:
            copy.wait()
    by_tap = [
        jnp.dot(jnp.concatenate(stack, axis=0), wt[3 * a], preferred_element_type=f32)
        for a, stack in enumerate((
            [ro[0], earlier[0], ro[4], ro[0], ro[6]],
            [ro[1], earlier[1], ro[5], ro[0], ro[7]],
            [ro[2], ro[4], ro[6], ro[0]],
        ))
    ]
    first_two = by_tap[0] + by_tap[1]
    whole = joined(first_two[0 : 3 * cols] + by_tap[2][0 : 3 * cols])
    own, aside = joined(first_two[3 * cols : 4 * cols]), joined(first_two[4 * cols : 5 * cols])
    z_most[...] = jnp.zeros_like(z_most)
    c_most[...] = jnp.zeros_like(c_most)
    encode(joined(by_tap[2][3 * cols : 4 * cols]) + jnp.where(opens[0], own, 0.0), z_send, row_of(0), z_most, 0)
    for k in (1, 2, 3):
        encode(whole[row_of(k - 1)], z_send, row_of(k), z_most, k)
    encode(aside, c_send, row_of(0), c_most, 0)

    ready(6)
    ready(7)
    taps(((0, 6), (1, 7)), p_raw)
    for r in range(half):
        encode(p_raw[row_of(r)], p_send, row_of(r), p_most, r)
    size = m_rows // 2
    halves = [pl.ds(i * size, size) for i in range(2)]
    sent = [
        (z_most, z_scale, at_tile(1)), (z_send, z_recv, at_tile(1)),
        (p_most, p_scale, at_tm(1)), (p_send.at[halves[0]], p_recv.at[halves[0]], at_tm(1)),
        (p_send.at[halves[1]], p_recv.at[halves[1]], at_tm(1)),
        (c_most, c_scale, aslant(1)), (c_send, c_recv, aslant(1)),
    ]
    halo = [remote(src, dst, halo_send.at[i], halo_recv.at[i], to) for i, (src, dst, to) in enumerate(sent)]
    pl.semaphore_wait(barrier, n_tile - 1 + len(reach) + 2)
    for copy in halo:
        copy.start()

    ready(0)
    ready(4)
    ready(5)
    taps(((2, 0),), y.at[0])
    taps(((0, 4), (1, 5), (2, 6)), y.at[3])

    ready(2)
    loads[3].wait()
    pair_columns(lambda r: jnp.where(opens[1], xb[4, r], xb[3, r]), 3)
    pair_columns(lambda r: jnp.where(opens[1], xb[4, r], xb[2, r]), 8)
    ready(1)
    taps(((0, 8), (1, 3), (2, 4)), y.at[2])
    taps(((0, 0), (1, 1), (2, 2)), y.at[1])

    def finish(k):
        above = decode(z_recv, row_of(k), z_scale, k)
        if k == 0:
            for copy in halo[2:]:
                copy.wait_recv()
            above = above + jnp.where(opens[0], 0.0, decode(c_recv, row_of(0), c_scale, 0))
            for r in range(half):
                there = row_of(r)
                y[0, there] = y[0, there] + jnp.where(opens[0], p_own[there], decode(p_recv, there, p_scale, r))
        y[k, 0:cols] = y[k, 0:cols] + jnp.where(tile == 0, 0.0, above)
        mean = jnp.sum(y[k], axis=0, keepdims=True) * (1.0 / m_rows)
        off = y[k] - mean
        return mean, jnp.sum(off * off, axis=0, keepdims=True)

    def pool(means, squares, count):
        mean = functools.reduce(jnp.add, means) * (1.0 / len(means))
        apart = functools.reduce(jnp.add, [(m - mean) * (m - mean) for m in means])
        return mean, functools.reduce(jnp.add, squares) + count * apart

    part = [None] * 4
    for copy in halo[:2]:
        copy.wait_recv()
    part[3] = finish(3)
    taps(((0, 0), (1, 0)), p_own)
    for k in (2, 1, 0):
        part[k] = finish(k)
    count = m_rows
    blocks = [pool([part[2 * m][0], part[2 * m + 1][0]], [part[2 * m][1], part[2 * m + 1][1]], count) for m in range(CH_DEV)]
    count *= 2

    fill = jnp.zeros((8 - 2 * CH_DEV, chans), f32)

    def packed(stats):
        return jnp.concatenate([s[0] for s in stats] + [s[1] for s in stats] + [fill], axis=0)

    mine[...] = packed(blocks)
    to_tiles = [
        remote(mine, from_tile.at[k - 1], as_sem.at[k - 1], ar_sem.at[k - 1], at_tile(k)) for k in around
    ]
    for copy in to_tiles:
        copy.start()
    for copy in to_tiles:
        copy.wait_recv()
    all_means = [mine[0:CH_DEV]] + [from_tile[k, 0:CH_DEV] for k in range(n_tile - 1)]
    all_squares = [mine[CH_DEV : 2 * CH_DEV]] + [from_tile[k, CH_DEV : 2 * CH_DEV] for k in range(n_tile - 1)]
    mean, square = pool(all_means, all_squares, count)
    count *= n_tile
    pooled[...] = jnp.concatenate([mean, square, fill], axis=0)

    to_tm = [remote(pooled, from_tm.at[i], bs_sem.at[i], br_sem.at[i], at_tm(k)) for i, k in enumerate(reach)]
    for copy in to_tm:
        copy.start()
    for copy in to_tm:
        copy.wait_recv()
    held = [(tm, pooled[...])] + [(tm - k, from_tm[i]) for i, k in enumerate(reach)]

    lane = lax.broadcasted_iota(jnp.int32, (1, chans), 1)

    def over_group(v):
        step = 1
        while step < GROUP:
            v = v + jnp.where((lane // step) % 2 == 1, pltpu.roll(v, step, 1), pltpu.roll(v, chans - step, 1))
            step *= 2
        return v

    rows_out = []
    for m in range(CH_DEV):
        shares = []
        for device, stats in held:
            for q in range(CH_DEV):
                slot = device * CH_DEV + q
                inside = jnp.logical_and(slot >= lows[m], slot < highs[m])
                shares.append((inside, stats[q : q + 1], stats[CH_DEV + q : CH_DEV + q + 1]))
        spans_here = jnp.full((1, chans), (highs[m] - lows[m]).astype(f32))
        clip_mean = functools.reduce(jnp.add, [jnp.where(i, a, 0.0) for i, a, _ in shares]) / spans_here
        mean = over_group(clip_mean) * (1.0 / GROUP)
        spread = functools.reduce(
            jnp.add, [jnp.where(i, s + count * ((a - mean) * (a - mean)), 0.0) for i, a, s in shares]
        )
        variance = over_group(spread) / (spans_here * float(count * GROUP))
        rows_out += [mean, lax.rsqrt(variance + EPS)]
    stat_out[...] = jnp.concatenate(rows_out + [fill], axis=0)

    for copy in halo + to_tiles + to_tm:
        copy.wait_send()


def finishing(y, stats, gain, bias, out_hbm, out, sem):
    copies = []
    for k in range(y.shape[0]):
        m = k // (F // 2)
        normed = (y[k] - stats[2 * m : 2 * m + 1]) * stats[2 * m + 1 : 2 * m + 2] * gain[...] + bias[...]
        halved = 0.5 * normed
        out[k] = (halved * jnp.tanh(halved) + halved).astype(bf16)
        copies.append(pltpu.make_async_copy(out.at[k], out_hbm.at[k], sem.at[k]))
        copies[-1].start()
    for copy in copies:
        copy.wait()


def body(input_frames, clip_spans, conv_weight, norm_gain, norm_bias):
    frames, rows, width, chans = input_frames.shape
    n_tm, n_tile = lax.axis_size("tm"), lax.axis_size("tile")
    half, cols = rows // 2, width // 2
    m_rows = half * cols
    outs = CH_DEV * (F // 2)
    weights = conv_weight.reshape(9, 3, chans, chans)
    n_reach = 2 * REACH
    dma = pltpu.SemaphoreType.DMA
    any_space, vmem = pl.BlockSpec(memory_space=pl.ANY), pl.BlockSpec(memory_space=pltpu.VMEM)
    y, stats = pl.pallas_call(
        functools.partial(kernel, n_tm, n_tile, rows, cols, chans),
        out_shape=[pltpu.VMEM((outs, m_rows, chans), f32), pltpu.VMEM((8, chans), f32)],
        in_specs=[any_space] * 3,
        out_specs=[vmem, vmem],
        scratch_shapes=[
            pltpu.SMEM(clip_spans.shape, jnp.int32),
            pltpu.VMEM((frames, width, chans), bf16),
            pltpu.VMEM((frames, cols, 2 * chans), bf16),
            pltpu.VMEM((frames, rows, width, chans), bf16),
            pltpu.VMEM((frames + 1, half, cols, 2 * chans), bf16),
            pltpu.VMEM((frames + 1, half + 1, cols, 2 * chans), bf16),
            pltpu.VMEM((9, 2 * chans, 2 * chans), bf16),
            pltpu.VMEM((m_rows, chans), f32),
            pltpu.VMEM((m_rows, chans), f32),
            *[
                pltpu.VMEM((n, chans), kind)
                for _ in range(2)
                for n, kind in (
                    (m_rows, jnp.int16), (half, f32), (cols, jnp.int16), (8, f32), (outs * cols, jnp.int16), (8, f32)
                )
            ],
            pltpu.VMEM((8, chans), f32),
            pltpu.VMEM((n_tile - 1, 8, chans), f32),
            pltpu.VMEM((8, chans), f32),
            pltpu.VMEM((n_reach, 8, chans), f32),
            dma, dma, dma((frames,)), dma((3, 3)), dma((7,)), dma((7,)),
            dma((n_tile - 1,)), dma((n_tile - 1,)), dma((n_reach,)), dma((n_reach,)),
        ],
        compiler_params=pltpu.CompilerParams(
            collective_id=0, has_side_effects=True, vmem_limit_bytes=48 * 2**20
        ),
    )(
        pltpu.with_memory_space_constraint(clip_spans, pltpu.HBM),
        input_frames,
        pltpu.with_memory_space_constraint(weights, pltpu.HBM),
    )
    out = pl.pallas_call(
        finishing,
        out_shape=jax.ShapeDtypeStruct((outs, m_rows, chans), bf16),
        in_specs=[vmem] * 4,
        out_specs=any_space,
        scratch_shapes=[pltpu.VMEM((outs, m_rows, chans), bf16), dma((outs,))],
        compiler_params=pltpu.CompilerParams(vmem_limit_bytes=16 * 2**20),
    )(
        pltpu.with_memory_space_constraint(y, pltpu.VMEM),
        pltpu.with_memory_space_constraint(stats, pltpu.VMEM),
        norm_gain.reshape(1, chans),
        norm_bias.reshape(1, chans),
    )
    return out.reshape(outs, half, cols, chans)


def solution(mesh):
    in_specs = (P("tm", "tile", None, None), P(), P(), P(), P())
    out_specs = P("tm", "tile", None, None)
    return jax.shard_map(body, mesh=mesh, in_specs=in_specs, out_specs=out_specs, check_vma=False)
```

```python
import functools

import jax
import jax.numpy as jnp
from jax import lax
from jax.experimental import pallas as pl
from jax.experimental.pallas import tpu as pltpu
from jax.sharding import PartitionSpec as P

F = 4
CH_DEV = 2
GROUP = 4
REACH = 4
EPS = 1e-6
CODES = 32767.0
TINY = 1e-30
MESH = pl.DeviceIdType.MESH
f32, bf16 = jnp.float32, jnp.bfloat16


def kernel(
    n_tm, n_tile, rows, cols, chans,
    spans_hbm, x_hbm, w_hbm, y, stat_out,
    spans, rb, ro, xb, xe, xo, wt, p_own, p_raw, p_send, p_most, c_send, c_most, z_send, z_most,
    p_recv, p_scale, c_recv, c_scale, z_recv, z_scale,
    mine, from_tile, pooled, from_tm,
    spans_sem, row_sem, in_sem, w_sem, halo_send, halo_recv, as_sem, ar_sem, bs_sem, br_sem,
):
    tm, tile = lax.axis_index("tm"), lax.axis_index("tile")
    half, c2 = rows // 2, 2 * chans
    m_rows = half * cols
    reach = [sign * k for k in range(REACH, 0, -1) for sign in (-1, 1)]
    around = sorted(range(1, n_tile), key=lambda k: -min(k, n_tile - k))

    def at_tm(k):
        return {"tm": lax.rem(tm + k + n_tm, n_tm)}

    def at_tile(k):
        return {"tile": lax.rem(tile + k + n_tile, n_tile)}

    def aslant(k):
        return at_tm(k) | at_tile(k)

    def has_tm(k):
        return jnp.logical_and(tm + k >= 0, tm + k < n_tm)

    def has_tile(k):
        return jnp.logical_and(tile + k >= 0, tile + k < n_tile)

    def has_both(k):
        return jnp.logical_and(has_tm(k), has_tile(k))

    def greet(there, to):
        @pl.when(there)
        def _():
            pl.semaphore_signal(barrier, inc=1, device_id=to, device_id_type=MESH)

    def start(copy, there):
        @pl.when(there)
        def _():
            copy.start()

    def wait_recv(copy, there):
        @pl.when(there)
        def _():
            copy.wait_recv()

    def wait_send(copy, there):
        @pl.when(there)
        def _():
            copy.wait_send()

    def remote(src, dst, send, recv, where):
        return pltpu.make_async_remote_copy(
            src_ref=src, dst_ref=dst, send_sem=send, recv_sem=recv, device_id=where, device_id_type=MESH
        )

    order = (6, 7, 0, 4, 5, 2, 3, 1)
    loads = {f: pltpu.make_async_copy(x_hbm.at[f], xb.at[f], in_sem.at[f]) for f in order}
    w_loads = []
    for a in range(3):
        from_w, to_w = w_hbm.at[3 * a : 3 * a + 3], wt.at[3 * a : 3 * a + 3]
        w_loads.append([
            pltpu.make_async_copy(from_w.at[:, 1], to_w.at[:, 0:chans, 0:chans], w_sem.at[a, 0]),
            pltpu.make_async_copy(from_w.at[:, 2], to_w.at[:, chans:c2, 0:chans], w_sem.at[a, 1]),
            pltpu.make_async_copy(from_w.at[:, 0], to_w.at[:, chans:c2, chans:c2], w_sem.at[a, 2]),
        ])
    spans_load = pltpu.make_async_copy(spans_hbm, spans, spans_sem)
    row_load = pltpu.make_async_copy(x_hbm.at[:, rows - 1], rb, row_sem)
    row_load.start()
    for a in range(3):
        for copy in w_loads[a]:
            copy.start()
    spans_load.start()
    for f in order:
        loads[f].start()

    for ref in (p_scale, c_scale, z_scale, from_tm):
        ref[...] = jnp.zeros_like(ref)

    barrier = pltpu.get_barrier_semaphore()
    met = jnp.int32(n_tile - 1)
    for k in around:
        pl.semaphore_signal(barrier, inc=1, device_id=at_tile(k), device_id_type=MESH)
    for k in reach:
        greet(has_tm(k), at_tm(k))
        met = met + has_tm(k).astype(jnp.int32)
    for k in (-1, 1):
        greet(has_both(k), aslant(k))
        met = met + has_both(k).astype(jnp.int32)

    spans_load.wait()
    ends, total = [], jnp.int32(0)
    for c in range(spans.shape[0]):
        total = total + spans[c]
        ends.append(total)
    lows, highs = [], []
    for m in range(CH_DEV):
        slot = tm * CH_DEV + m
        lo, hi = jnp.int32(0), jnp.int32(n_tm * CH_DEV)
        for end in ends:
            lo = jnp.maximum(lo, jnp.where(end <= slot, end, 0))
            hi = jnp.minimum(hi, jnp.where(end > slot, end, n_tm * CH_DEV))
        lows.append(lo)
        highs.append(hi)
    opens = [(lows[m] == tm * CH_DEV + m) for m in range(CH_DEV)]

    wt[:, 0:chans, chans:c2] = jnp.zeros((wt.shape[0], chans, chans), bf16)
    for f in range(xo.shape[0]):
        xo[f, 0] = jnp.zeros((cols, c2), bf16)

    def pair_columns(raw, f):
        for r in range(rows):
            pair = raw(r).reshape(cols, c2)
            if r % 2:
                xo[f, 1 + r // 2] = pair
            else:
                xe[f, r // 2] = pair

    def joined(both):
        moved = pltpu.roll(both[:, chans:c2], 1, 0)
        column = lax.broadcasted_iota(jnp.int32, moved.shape, 0) % cols
        return both[:, 0:chans] + jnp.where(column == 0, 0.0, moved)

    def taps(pairs, into, add=False):
        step = half // 2
        for part in range(2):
            first = part * step
            sums = None
            for a, f in pairs:
                for b, lhs in ((0, xo[f, first : first + step]), (1, xe[f, first : first + step]),
                               (2, xo[f, first + 1 : first + 1 + step])):
                    one = jnp.dot(lhs.reshape(step * cols, c2), wt[3 * a + b], preferred_element_type=f32)
                    sums = one if sums is None else sums + one
            there = slice(first * cols, (first + step) * cols)
            into[there] = into[there] + joined(sums) if add else joined(sums)

    def encode(value, codes, there, most, r):
        top = jnp.maximum(jnp.max(jnp.abs(value), axis=0, keepdims=True), TINY)
        most[r : r + 1] = top
        codes[there] = jnp.round(value * (CODES / top)).astype(jnp.int32).astype(jnp.int16)

    def decode(codes, there, most, r):
        return codes[there].astype(jnp.int32).astype(f32) * (most[r : r + 1] * (1.0 / CODES))

    def row_of(r):
        return slice(r * cols, (r + 1) * cols)

    def ready(f):
        loads[f].wait()
        pair_columns(lambda r: xb[f, r], f)

    def w_ready(a):
        for copy in w_loads[a]:
            copy.wait()

    row_load.wait()
    for f in range(xb.shape[0]):
        ro[f] = rb[f].reshape(cols, c2)
    earlier = [jnp.where(opens[1], ro[4], ro[f]) for f in (2, 3)]
    for a in range(3):
        for copy in w_loads[a]:
            copy.wait()
    by_tap = [
        jnp.dot(jnp.concatenate(stack, axis=0), wt[3 * a], preferred_element_type=f32)
        for a, stack in enumerate((
            [ro[0], earlier[0], ro[4], ro[0], ro[6]],
            [ro[1], earlier[1], ro[5], ro[0], ro[7]],
            [ro[2], ro[4], ro[6], ro[0]],
        ))
    ]
    first_two = by_tap[0] + by_tap[1]
    whole = joined(first_two[0 : 3 * cols] + by_tap[2][0 : 3 * cols])
    own, aside = joined(first_two[3 * cols : 4 * cols]), joined(first_two[4 * cols : 5 * cols])
    z_most[...] = jnp.zeros_like(z_most)
    c_most[...] = jnp.zeros_like(c_most)
    encode(joined(by_tap[2][3 * cols : 4 * cols]) + jnp.where(opens[0], own, 0.0), z_send, row_of(0), z_most, 0)
    for k in (1, 2, 3):
        encode(whole[row_of(k - 1)], z_send, row_of(k), z_most, k)
    encode(aside, c_send, row_of(0), c_most, 0)

    ready(6)
    ready(7)
    taps(((0, 6), (1, 7)), p_raw)
    for r in range(half):
        encode(p_raw[row_of(r)], p_send, row_of(r), p_most, r)
    size = m_rows // 2
    halves = [pl.ds(i * size, size) for i in range(2)]
    above_on, last_on, corner_on = ((has_tile(1), has_tile(-1)), (has_tm(1), has_tm(-1)), (has_both(1), has_both(-1)))
    sent = [
        (z_most, z_scale, at_tile(1), above_on), (z_send, z_recv, at_tile(1), above_on),
        (p_most, p_scale, at_tm(1), last_on), (p_send.at[halves[0]], p_recv.at[halves[0]], at_tm(1), last_on),
        (p_send.at[halves[1]], p_recv.at[halves[1]], at_tm(1), last_on),
        (c_most, c_scale, aslant(1), corner_on), (c_send, c_recv, aslant(1), corner_on),
    ]
    halo = [
        (remote(src, dst, halo_send.at[i], halo_recv.at[i], to), *on) for i, (src, dst, to, on) in enumerate(sent)
    ]
    pl.semaphore_wait(barrier, met)
    for copy, out_on, _ in halo:
        start(copy, out_on)

    ready(0)
    ready(4)
    ready(5)
    taps(((2, 0),), y.at[0])
    taps(((0, 4), (1, 5), (2, 6)), y.at[3])

    ready(2)
    loads[3].wait()
    pair_columns(lambda r: jnp.where(opens[1], xb[4, r], xb[3, r]), 3)
    pair_columns(lambda r: jnp.where(opens[1], xb[4, r], xb[2, r]), 8)
    ready(1)
    taps(((0, 8), (1, 3), (2, 4)), y.at[2])
    taps(((0, 0), (1, 1), (2, 2)), y.at[1])

    def finish(k):
        above = decode(z_recv, row_of(k), z_scale, k)
        if k == 0:
            for copy, _, in_on in halo[2:]:
                wait_recv(copy, in_on)
            above = above + jnp.where(opens[0], 0.0, decode(c_recv, row_of(0), c_scale, 0))
            for r in range(half):
                there = row_of(r)
                y[0, there] = y[0, there] + jnp.where(opens[0], p_own[there], decode(p_recv, there, p_scale, r))
        y[k, 0:cols] = y[k, 0:cols] + jnp.where(tile == 0, 0.0, above)
        mean = jnp.sum(y[k], axis=0, keepdims=True) * (1.0 / m_rows)
        off = y[k] - mean
        return mean, jnp.sum(off * off, axis=0, keepdims=True)

    def pool(means, squares, count):
        mean = functools.reduce(jnp.add, means) * (1.0 / len(means))
        apart = functools.reduce(jnp.add, [(m - mean) * (m - mean) for m in means])
        return mean, functools.reduce(jnp.add, squares) + count * apart

    part = [None] * 4
    for copy, _, in_on in halo[:2]:
        wait_recv(copy, in_on)
    part[3] = finish(3)
    taps(((0, 0), (1, 0)), p_own)
    for k in (2, 1, 0):
        part[k] = finish(k)
    count = m_rows
    blocks = [pool([part[2 * m][0], part[2 * m + 1][0]], [part[2 * m][1], part[2 * m + 1][1]], count) for m in range(CH_DEV)]
    count *= 2

    fill = jnp.zeros((8 - 2 * CH_DEV, chans), f32)

    def packed(stats):
        return jnp.concatenate([s[0] for s in stats] + [s[1] for s in stats] + [fill], axis=0)

    mine[...] = packed(blocks)
    to_tiles = [
        remote(mine, from_tile.at[k - 1], as_sem.at[k - 1], ar_sem.at[k - 1], at_tile(k)) for k in around
    ]
    for copy in to_tiles:
        copy.start()
    for copy in to_tiles:
        copy.wait_recv()
    all_means = [mine[0:CH_DEV]] + [from_tile[k, 0:CH_DEV] for k in range(n_tile - 1)]
    all_squares = [mine[CH_DEV : 2 * CH_DEV]] + [from_tile[k, CH_DEV : 2 * CH_DEV] for k in range(n_tile - 1)]
    mean, square = pool(all_means, all_squares, count)
    count *= n_tile
    pooled[...] = jnp.concatenate([mean, square, fill], axis=0)

    to_tm = [remote(pooled, from_tm.at[i], bs_sem.at[i], br_sem.at[i], at_tm(k)) for i, k in enumerate(reach)]
    for copy, k in zip(to_tm, reach):
        start(copy, has_tm(k))
    for copy, k in zip(to_tm, reach):
        wait_recv(copy, has_tm(-k))
    held = [(tm, pooled[...])] + [(tm - k, from_tm[i]) for i, k in enumerate(reach)]

    lane = lax.broadcasted_iota(jnp.int32, (1, chans), 1)

    def over_group(v):
        step = 1
        while step < GROUP:
            v = v + jnp.where((lane // step) % 2 == 1, pltpu.roll(v, step, 1), pltpu.roll(v, chans - step, 1))
            step *= 2
        return v

    rows_out = []
    for m in range(CH_DEV):
        shares = []
        for device, stats in held:
            for q in range(CH_DEV):
                slot = device * CH_DEV + q
                inside = jnp.logical_and(slot >= lows[m], slot < highs[m])
                shares.append((inside, stats[q : q + 1], stats[CH_DEV + q : CH_DEV + q + 1]))
        spans_here = jnp.full((1, chans), (highs[m] - lows[m]).astype(f32))
        clip_mean = functools.reduce(jnp.add, [jnp.where(i, a, 0.0) for i, a, _ in shares]) / spans_here
        mean = over_group(clip_mean) * (1.0 / GROUP)
        spread = functools.reduce(
            jnp.add, [jnp.where(i, s + count * ((a - mean) * (a - mean)), 0.0) for i, a, s in shares]
        )
        variance = over_group(spread) / (spans_here * float(count * GROUP))
        rows_out += [mean, lax.rsqrt(variance + EPS)]
    stat_out[...] = jnp.concatenate(rows_out + [fill], axis=0)

    for copy, out_on, _ in halo:
        wait_send(copy, out_on)
    for copy in to_tiles:
        copy.wait_send()
    for copy, k in zip(to_tm, reach):
        wait_send(copy, has_tm(k))


def finishing(y, stats, gain, bias, out_hbm, out, sem):
    copies = []
    for k in range(y.shape[0]):
        m = k // (F // 2)
        normed = (y[k] - stats[2 * m : 2 * m + 1]) * stats[2 * m + 1 : 2 * m + 2] * gain[...] + bias[...]
        halved = 0.5 * normed
        out[k] = (halved * jnp.tanh(halved) + halved).astype(bf16)
        copies.append(pltpu.make_async_copy(out.at[k], out_hbm.at[k], sem.at[k]))
        copies[-1].start()
    for copy in copies:
        copy.wait()


def body(input_frames, clip_spans, conv_weight, norm_gain, norm_bias):
    frames, rows, width, chans = input_frames.shape
    n_tm, n_tile = lax.axis_size("tm"), lax.axis_size("tile")
    half, cols = rows // 2, width // 2
    m_rows = half * cols
    outs = CH_DEV * (F // 2)
    weights = conv_weight.reshape(9, 3, chans, chans)
    n_reach = 2 * REACH
    dma = pltpu.SemaphoreType.DMA
    any_space, vmem = pl.BlockSpec(memory_space=pl.ANY), pl.BlockSpec(memory_space=pltpu.VMEM)
    y, stats = pl.pallas_call(
        functools.partial(kernel, n_tm, n_tile, rows, cols, chans),
        out_shape=[pltpu.VMEM((outs, m_rows, chans), f32), pltpu.VMEM((8, chans), f32)],
        in_specs=[any_space] * 3,
        out_specs=[vmem, vmem],
        scratch_shapes=[
            pltpu.SMEM(clip_spans.shape, jnp.int32),
            pltpu.VMEM((frames, width, chans), bf16),
            pltpu.VMEM((frames, cols, 2 * chans), bf16),
            pltpu.VMEM((frames, rows, width, chans), bf16),
            pltpu.VMEM((frames + 1, half, cols, 2 * chans), bf16),
            pltpu.VMEM((frames + 1, half + 1, cols, 2 * chans), bf16),
            pltpu.VMEM((9, 2 * chans, 2 * chans), bf16),
            pltpu.VMEM((m_rows, chans), f32),
            pltpu.VMEM((m_rows, chans), f32),
            *[
                pltpu.VMEM((n, chans), kind)
                for _ in range(2)
                for n, kind in (
                    (m_rows, jnp.int16), (half, f32), (cols, jnp.int16), (8, f32), (outs * cols, jnp.int16), (8, f32)
                )
            ],
            pltpu.VMEM((8, chans), f32),
            pltpu.VMEM((n_tile - 1, 8, chans), f32),
            pltpu.VMEM((8, chans), f32),
            pltpu.VMEM((n_reach, 8, chans), f32),
            dma, dma, dma((frames,)), dma((3, 3)), dma((7,)), dma((7,)),
            dma((n_tile - 1,)), dma((n_tile - 1,)), dma((n_reach,)), dma((n_reach,)),
        ],
        compiler_params=pltpu.CompilerParams(
            collective_id=0, has_side_effects=True, vmem_limit_bytes=48 * 2**20
        ),
    )(
        pltpu.with_memory_space_constraint(clip_spans, pltpu.HBM),
        input_frames,
        pltpu.with_memory_space_constraint(weights, pltpu.HBM),
    )
    out = pl.pallas_call(
        finishing,
        out_shape=jax.ShapeDtypeStruct((outs, m_rows, chans), bf16),
        in_specs=[vmem] * 4,
        out_specs=any_space,
        scratch_shapes=[pltpu.VMEM((outs, m_rows, chans), bf16), dma((outs,))],
        compiler_params=pltpu.CompilerParams(vmem_limit_bytes=16 * 2**20),
    )(
        pltpu.with_memory_space_constraint(y, pltpu.VMEM),
        pltpu.with_memory_space_constraint(stats, pltpu.VMEM),
        norm_gain.reshape(1, chans),
        norm_bias.reshape(1, chans),
    )
    return out.reshape(outs, half, cols, chans)


def solution(mesh):
    in_specs = (P("tm", "tile", None, None), P(), P(), P(), P())
    out_specs = P("tm", "tile", None, None)
    return jax.shard_map(body, mesh=mesh, in_specs=in_specs, out_specs=out_specs, check_vma=False)
```

```python
import functools

import jax
import jax.numpy as jnp
from jax import lax
from jax.experimental import pallas as pl
from jax.experimental.pallas import tpu as pltpu
from jax.sharding import PartitionSpec as P

F = 4
CH_DEV = 2
GROUP = 4
REACH = 4
EPS = 1e-6
CODES = 32767.0
TINY = 1e-30
MESH = pl.DeviceIdType.MESH
f32, bf16 = jnp.float32, jnp.bfloat16


def kernel(
    n_tm, n_tile, rows, cols, chans,
    spans_hbm, x_hbm, w_hbm, y, stat_out,
    spans, rb, ro, xb, xe, xo, wt, p_own, p_raw, p_send, p_most, c_send, c_most, z_send, z_most,
    p_recv, p_scale, c_recv, c_scale, z_recv, z_scale,
    mine, from_tile, pooled, from_tm,
    spans_sem, row_sem, in_sem, w_sem, halo_send, halo_recv, as_sem, ar_sem, bs_sem, br_sem,
):
    tm, tile = lax.axis_index("tm"), lax.axis_index("tile")
    half, c2 = rows // 2, 2 * chans
    m_rows = half * cols
    reach = [sign * k for k in range(REACH, 0, -1) for sign in (-1, 1)]
    around = sorted(range(1, n_tile), key=lambda k: -min(k, n_tile - k))

    def at_tm(k):
        return {"tm": lax.rem(tm + k + n_tm, n_tm)}

    def at_tile(k):
        return {"tile": lax.rem(tile + k + n_tile, n_tile)}

    def aslant(k):
        return at_tm(k) | at_tile(k)

    def has_tm(k):
        return jnp.logical_and(tm + k >= 0, tm + k < n_tm)

    def has_tile(k):
        return jnp.logical_and(tile + k >= 0, tile + k < n_tile)

    def has_both(k):
        return jnp.logical_and(has_tm(k), has_tile(k))

    def greet(there, to):
        @pl.when(there)
        def _():
            pl.semaphore_signal(barrier, inc=1, device_id=to, device_id_type=MESH)

    def start(copy, there):
        @pl.when(there)
        def _():
            copy.start()

    def wait_recv(copy, there):
        @pl.when(there)
        def _():
            copy.wait_recv()

    def wait_send(copy, there):
        @pl.when(there)
        def _():
            copy.wait_send()

    def remote(src, dst, send, recv, where):
        return pltpu.make_async_remote_copy(
            src_ref=src, dst_ref=dst, send_sem=send, recv_sem=recv, device_id=where, device_id_type=MESH
        )

    order = (6, 7, 0, 4, 5, 2, 3, 1)
    loads = {f: pltpu.make_async_copy(x_hbm.at[f], xb.at[f], in_sem.at[f]) for f in order}
    w_loads = []
    for a in range(3):
        from_w, to_w = w_hbm.at[3 * a : 3 * a + 3], wt.at[3 * a : 3 * a + 3]
        w_loads.append([
            pltpu.make_async_copy(from_w.at[:, 1], to_w.at[:, 0:chans, 0:chans], w_sem.at[a, 0]),
            pltpu.make_async_copy(from_w.at[:, 2], to_w.at[:, chans:c2, 0:chans], w_sem.at[a, 1]),
            pltpu.make_async_copy(from_w.at[:, 0], to_w.at[:, chans:c2, chans:c2], w_sem.at[a, 2]),
        ])
    spans_load = pltpu.make_async_copy(spans_hbm, spans, spans_sem)
    row_load = pltpu.make_async_copy(x_hbm.at[:, rows - 1], rb, row_sem)
    row_load.start()
    for a in range(3):
        for copy in w_loads[a]:
            copy.start()
    spans_load.start()
    for f in order:
        loads[f].start()

    for ref in (p_scale, c_scale, z_scale, from_tm):
        ref[...] = jnp.zeros_like(ref)

    barrier = pltpu.get_barrier_semaphore()
    met = jnp.int32(n_tile - 1)
    for k in around:
        pl.semaphore_signal(barrier, inc=1, device_id=at_tile(k), device_id_type=MESH)
    for k in reach:
        greet(has_tm(k), at_tm(k))
        met = met + has_tm(k).astype(jnp.int32)
    for k in (-1, 1):
        greet(has_both(k), aslant(k))
        met = met + has_both(k).astype(jnp.int32)

    spans_load.wait()
    ends, total = [], jnp.int32(0)
    for c in range(spans.shape[0]):
        total = total + spans[c]
        ends.append(total)
    lows, highs = [], []
    for m in range(CH_DEV):
        slot = tm * CH_DEV + m
        lo, hi = jnp.int32(0), jnp.int32(n_tm * CH_DEV)
        for end in ends:
            lo = jnp.maximum(lo, jnp.where(end <= slot, end, 0))
            hi = jnp.minimum(hi, jnp.where(end > slot, end, n_tm * CH_DEV))
        lows.append(lo)
        highs.append(hi)
    opens = [(lows[m] == tm * CH_DEV + m) for m in range(CH_DEV)]

    wt[:, 0:chans, chans:c2] = jnp.zeros((wt.shape[0], chans, chans), bf16)
    for f in range(xo.shape[0]):
        xo[f, 0] = jnp.zeros((cols, c2), bf16)

    def pair_columns(raw, f):
        for r in range(rows):
            pair = raw(r).reshape(cols, c2)
            if r % 2:
                xo[f, 1 + r // 2] = pair
            else:
                xe[f, r // 2] = pair

    def joined(both):
        moved = pltpu.roll(both[:, chans:c2], 1, 0)
        column = lax.broadcasted_iota(jnp.int32, moved.shape, 0) % cols
        return both[:, 0:chans] + jnp.where(column == 0, 0.0, moved)

    def taps(pairs, into, add=False):
        step = half // 2
        for part in range(2):
            first = part * step
            sums = None
            for a, f in pairs:
                for b, lhs in ((0, xo[f, first : first + step]), (1, xe[f, first : first + step]),
                               (2, xo[f, first + 1 : first + 1 + step])):
                    one = jnp.dot(lhs.reshape(step * cols, c2), wt[3 * a + b], preferred_element_type=f32)
                    sums = one if sums is None else sums + one
            there = slice(first * cols, (first + step) * cols)
            into[there] = into[there] + joined(sums) if add else joined(sums)

    def encode(value, codes, there, most, r):
        top = jnp.maximum(jnp.max(jnp.abs(value), axis=0, keepdims=True), TINY)
        most[r : r + 1] = top
        codes[there] = jnp.round(value * (CODES / top)).astype(jnp.int32).astype(jnp.int16)

    def decode(codes, there, most, r):
        return codes[there].astype(jnp.int32).astype(f32) * (most[r : r + 1] * (1.0 / CODES))

    def row_of(r):
        return slice(r * cols, (r + 1) * cols)

    def ready(f):
        loads[f].wait()
        pair_columns(lambda r: xb[f, r], f)

    def w_ready(a):
        for copy in w_loads[a]:
            copy.wait()

    row_load.wait()
    for f in range(xb.shape[0]):
        ro[f] = rb[f].reshape(cols, c2)
    earlier = [jnp.where(opens[1], ro[4], ro[f]) for f in (2, 3)]
    for a in range(3):
        for copy in w_loads[a]:
            copy.wait()
    by_tap = [
        jnp.dot(jnp.concatenate(stack, axis=0), wt[3 * a], preferred_element_type=f32)
        for a, stack in enumerate((
            [ro[0], earlier[0], ro[4], ro[0], ro[6]],
            [ro[1], earlier[1], ro[5], ro[0], ro[7]],
            [ro[2], ro[4], ro[6], ro[0]],
        ))
    ]
    first_two = by_tap[0] + by_tap[1]
    whole = joined(first_two[0 : 3 * cols] + by_tap[2][0 : 3 * cols])
    own, aside = joined(first_two[3 * cols : 4 * cols]), joined(first_two[4 * cols : 5 * cols])
    z_most[...] = jnp.zeros_like(z_most)
    c_most[...] = jnp.zeros_like(c_most)
    encode(joined(by_tap[2][3 * cols : 4 * cols]) + jnp.where(opens[0], own, 0.0), z_send, row_of(0), z_most, 0)
    for k in (1, 2, 3):
        encode(whole[row_of(k - 1)], z_send, row_of(k), z_most, k)
    encode(aside, c_send, row_of(0), c_most, 0)

    ready(6)
    taps(((0, 6),), p_raw)
    ready(7)
    taps(((1, 7),), p_raw, add=True)
    for r in range(half):
        encode(p_raw[row_of(r)], p_send, row_of(r), p_most, r)
    size = m_rows // 2
    halves = [pl.ds(i * size, size) for i in range(2)]
    above_on, last_on, corner_on = ((has_tile(1), has_tile(-1)), (has_tm(1), has_tm(-1)), (has_both(1), has_both(-1)))
    sent = [
        (z_most, z_scale, at_tile(1), above_on), (z_send, z_recv, at_tile(1), above_on),
        (p_most, p_scale, at_tm(1), last_on), (p_send.at[halves[0]], p_recv.at[halves[0]], at_tm(1), last_on),
        (p_send.at[halves[1]], p_recv.at[halves[1]], at_tm(1), last_on),
        (c_most, c_scale, aslant(1), corner_on), (c_send, c_recv, aslant(1), corner_on),
    ]
    halo = [
        (remote(src, dst, halo_send.at[i], halo_recv.at[i], to), *on) for i, (src, dst, to, on) in enumerate(sent)
    ]
    pl.semaphore_wait(barrier, met)
    for copy, out_on, _ in halo:
        start(copy, out_on)

    ready(0)
    ready(4)
    ready(5)
    taps(((2, 0),), y.at[0])
    taps(((0, 0),), p_own)
    taps(((0, 4), (1, 5), (2, 6)), y.at[3])

    ready(2)
    loads[3].wait()
    pair_columns(lambda r: jnp.where(opens[1], xb[4, r], xb[3, r]), 3)
    pair_columns(lambda r: jnp.where(opens[1], xb[4, r], xb[2, r]), 8)
    ready(1)
    taps(((0, 8), (1, 3), (2, 4)), y.at[2])
    y[1] = p_own[...]
    taps(((1, 1), (2, 2)), y.at[1], add=True)

    def finish(k):
        above = decode(z_recv, row_of(k), z_scale, k)
        if k == 0:
            for copy, _, in_on in halo[2:]:
                wait_recv(copy, in_on)
            above = above + jnp.where(opens[0], 0.0, decode(c_recv, row_of(0), c_scale, 0))
            for r in range(half):
                there = row_of(r)
                y[0, there] = y[0, there] + jnp.where(opens[0], p_own[there], decode(p_recv, there, p_scale, r))
        y[k, 0:cols] = y[k, 0:cols] + jnp.where(tile == 0, 0.0, above)
        mean = jnp.sum(y[k], axis=0, keepdims=True) * (1.0 / m_rows)
        off = y[k] - mean
        return mean, jnp.sum(off * off, axis=0, keepdims=True)

    def pool(means, squares, count):
        mean = functools.reduce(jnp.add, means) * (1.0 / len(means))
        apart = functools.reduce(jnp.add, [(m - mean) * (m - mean) for m in means])
        return mean, functools.reduce(jnp.add, squares) + count * apart

    part = [None] * 4
    for copy, _, in_on in halo[:2]:
        wait_recv(copy, in_on)
    part[3] = finish(3)
    taps(((1, 0),), p_own, add=True)
    for k in (2, 1, 0):
        part[k] = finish(k)
    count = m_rows
    blocks = [pool([part[2 * m][0], part[2 * m + 1][0]], [part[2 * m][1], part[2 * m + 1][1]], count) for m in range(CH_DEV)]
    count *= 2

    fill = jnp.zeros((8 - 2 * CH_DEV, chans), f32)

    def packed(stats):
        return jnp.concatenate([s[0] for s in stats] + [s[1] for s in stats] + [fill], axis=0)

    mine[...] = packed(blocks)
    to_tiles = [
        remote(mine, from_tile.at[k - 1], as_sem.at[k - 1], ar_sem.at[k - 1], at_tile(k)) for k in around
    ]
    for copy in to_tiles:
        copy.start()
    for copy in to_tiles:
        copy.wait_recv()
    all_means = [mine[0:CH_DEV]] + [from_tile[k, 0:CH_DEV] for k in range(n_tile - 1)]
    all_squares = [mine[CH_DEV : 2 * CH_DEV]] + [from_tile[k, CH_DEV : 2 * CH_DEV] for k in range(n_tile - 1)]
    mean, square = pool(all_means, all_squares, count)
    count *= n_tile
    pooled[...] = jnp.concatenate([mean, square, fill], axis=0)

    to_tm = [remote(pooled, from_tm.at[i], bs_sem.at[i], br_sem.at[i], at_tm(k)) for i, k in enumerate(reach)]
    for copy, k in zip(to_tm, reach):
        start(copy, has_tm(k))
    for copy, k in zip(to_tm, reach):
        wait_recv(copy, has_tm(-k))
    held = [(tm, pooled[...])] + [(tm - k, from_tm[i]) for i, k in enumerate(reach)]

    lane = lax.broadcasted_iota(jnp.int32, (1, chans), 1)

    def over_group(v):
        step = 1
        while step < GROUP:
            v = v + jnp.where((lane // step) % 2 == 1, pltpu.roll(v, step, 1), pltpu.roll(v, chans - step, 1))
            step *= 2
        return v

    rows_out = []
    for m in range(CH_DEV):
        shares = []
        for device, stats in held:
            for q in range(CH_DEV):
                slot = device * CH_DEV + q
                inside = jnp.logical_and(slot >= lows[m], slot < highs[m])
                shares.append((inside, stats[q : q + 1], stats[CH_DEV + q : CH_DEV + q + 1]))
        spans_here = jnp.full((1, chans), (highs[m] - lows[m]).astype(f32))
        clip_mean = functools.reduce(jnp.add, [jnp.where(i, a, 0.0) for i, a, _ in shares]) / spans_here
        mean = over_group(clip_mean) * (1.0 / GROUP)
        spread = functools.reduce(
            jnp.add, [jnp.where(i, s + count * ((a - mean) * (a - mean)), 0.0) for i, a, s in shares]
        )
        variance = over_group(spread) / (spans_here * float(count * GROUP))
        rows_out += [mean, lax.rsqrt(variance + EPS)]
    stat_out[...] = jnp.concatenate(rows_out + [fill], axis=0)

    for copy, out_on, _ in halo:
        wait_send(copy, out_on)
    for copy in to_tiles:
        copy.wait_send()
    for copy, k in zip(to_tm, reach):
        wait_send(copy, has_tm(k))


def finishing(y, stats, gain, bias, out_hbm, out, sem):
    copies = []
    for k in range(y.shape[0]):
        m = k // (F // 2)
        normed = (y[k] - stats[2 * m : 2 * m + 1]) * stats[2 * m + 1 : 2 * m + 2] * gain[...] + bias[...]
        halved = 0.5 * normed
        out[k] = (halved * jnp.tanh(halved) + halved).astype(bf16)
        copies.append(pltpu.make_async_copy(out.at[k], out_hbm.at[k], sem.at[k]))
        copies[-1].start()
    for copy in copies:
        copy.wait()


def body(input_frames, clip_spans, conv_weight, norm_gain, norm_bias):
    frames, rows, width, chans = input_frames.shape
    n_tm, n_tile = lax.axis_size("tm"), lax.axis_size("tile")
    half, cols = rows // 2, width // 2
    m_rows = half * cols
    outs = CH_DEV * (F // 2)
    weights = conv_weight.reshape(9, 3, chans, chans)
    n_reach = 2 * REACH
    dma = pltpu.SemaphoreType.DMA
    any_space, vmem = pl.BlockSpec(memory_space=pl.ANY), pl.BlockSpec(memory_space=pltpu.VMEM)
    y, stats = pl.pallas_call(
        functools.partial(kernel, n_tm, n_tile, rows, cols, chans),
        out_shape=[pltpu.VMEM((outs, m_rows, chans), f32), pltpu.VMEM((8, chans), f32)],
        in_specs=[any_space] * 3,
        out_specs=[vmem, vmem],
        scratch_shapes=[
            pltpu.SMEM(clip_spans.shape, jnp.int32),
            pltpu.VMEM((frames, width, chans), bf16),
            pltpu.VMEM((frames, cols, 2 * chans), bf16),
            pltpu.VMEM((frames, rows, width, chans), bf16),
            pltpu.VMEM((frames + 1, half, cols, 2 * chans), bf16),
            pltpu.VMEM((frames + 1, half + 1, cols, 2 * chans), bf16),
            pltpu.VMEM((9, 2 * chans, 2 * chans), bf16),
            pltpu.VMEM((m_rows, chans), f32),
            pltpu.VMEM((m_rows, chans), f32),
            *[
                pltpu.VMEM((n, chans), kind)
                for _ in range(2)
                for n, kind in (
                    (m_rows, jnp.int16), (half, f32), (cols, jnp.int16), (8, f32), (outs * cols, jnp.int16), (8, f32)
                )
            ],
            pltpu.VMEM((8, chans), f32),
            pltpu.VMEM((n_tile - 1, 8, chans), f32),
            pltpu.VMEM((8, chans), f32),
            pltpu.VMEM((n_reach, 8, chans), f32),
            dma, dma, dma((frames,)), dma((3, 3)), dma((7,)), dma((7,)),
            dma((n_tile - 1,)), dma((n_tile - 1,)), dma((n_reach,)), dma((n_reach,)),
        ],
        compiler_params=pltpu.CompilerParams(
            collective_id=0, has_side_effects=True, vmem_limit_bytes=48 * 2**20
        ),
    )(
        pltpu.with_memory_space_constraint(clip_spans, pltpu.HBM),
        input_frames,
        pltpu.with_memory_space_constraint(weights, pltpu.HBM),
    )
    out = pl.pallas_call(
        finishing,
        out_shape=jax.ShapeDtypeStruct((outs, m_rows, chans), bf16),
        in_specs=[vmem] * 4,
        out_specs=any_space,
        scratch_shapes=[pltpu.VMEM((outs, m_rows, chans), bf16), dma((outs,))],
        compiler_params=pltpu.CompilerParams(vmem_limit_bytes=16 * 2**20),
    )(
        pltpu.with_memory_space_constraint(y, pltpu.VMEM),
        pltpu.with_memory_space_constraint(stats, pltpu.VMEM),
        norm_gain.reshape(1, chans),
        norm_bias.reshape(1, chans),
    )
    return out.reshape(outs, half, cols, chans)


def solution(mesh):
    in_specs = (P("tm", "tile", None, None), P(), P(), P(), P())
    out_specs = P("tm", "tile", None, None)
    return jax.shard_map(body, mesh=mesh, in_specs=in_specs, out_specs=out_specs, check_vma=False)
```

```python
import functools

import jax
import jax.numpy as jnp
from jax import lax
from jax.experimental import pallas as pl
from jax.experimental.pallas import tpu as pltpu
from jax.sharding import PartitionSpec as P

F = 4
CH_DEV = 2
GROUP = 4
REACH = 4
EPS = 1e-6
CODES = 32767.0
TINY = 1e-30
MESH = pl.DeviceIdType.MESH
f32, bf16 = jnp.float32, jnp.bfloat16


def kernel(
    n_tm, n_tile, rows, cols, chans,
    spans_hbm, x_hbm, w_hbm, y, stat_out,
    spans, rb, ro, xb, xe, xo, wt, p_own, p_raw, p_send, p_most, c_send, c_most, z_send, z_most,
    p_recv, p_scale, c_recv, c_scale, z_recv, z_scale,
    mine, from_tile, pooled, from_tm,
    spans_sem, row_sem, in_sem, w_sem, halo_send, halo_recv, as_sem, ar_sem, bs_sem, br_sem,
):
    tm, tile = lax.axis_index("tm"), lax.axis_index("tile")
    half, c2 = rows // 2, 2 * chans
    m_rows = half * cols
    reach = [sign * k for k in range(REACH, 0, -1) for sign in (-1, 1)]
    around = sorted(range(1, n_tile), key=lambda k: -min(k, n_tile - k))

    def at_tm(k):
        return {"tm": lax.rem(tm + k + n_tm, n_tm)}

    def at_tile(k):
        return {"tile": lax.rem(tile + k + n_tile, n_tile)}

    def aslant(k):
        return at_tm(k) | at_tile(k)

    def has_tm(k):
        return jnp.logical_and(tm + k >= 0, tm + k < n_tm)

    def has_tile(k):
        return jnp.logical_and(tile + k >= 0, tile + k < n_tile)

    def has_both(k):
        return jnp.logical_and(has_tm(k), has_tile(k))

    def greet(there, to):
        @pl.when(there)
        def _():
            pl.semaphore_signal(barrier, inc=1, device_id=to, device_id_type=MESH)

    def start(copy, there):
        @pl.when(there)
        def _():
            copy.start()

    def wait_recv(copy, there):
        @pl.when(there)
        def _():
            copy.wait_recv()

    def wait_send(copy, there):
        @pl.when(there)
        def _():
            copy.wait_send()

    def remote(src, dst, send, recv, where):
        return pltpu.make_async_remote_copy(
            src_ref=src, dst_ref=dst, send_sem=send, recv_sem=recv, device_id=where, device_id_type=MESH
        )

    order = (6, 7, 0, 4, 5, 2, 3, 1)
    loads = {f: pltpu.make_async_copy(x_hbm.at[f], xb.at[f], in_sem.at[f]) for f in order}
    w_loads = []
    for a in range(3):
        from_w, to_w = w_hbm.at[3 * a : 3 * a + 3], wt.at[3 * a : 3 * a + 3]
        w_loads.append([
            pltpu.make_async_copy(from_w.at[:, 1], to_w.at[:, 0:chans, 0:chans], w_sem.at[a, 0]),
            pltpu.make_async_copy(from_w.at[:, 2], to_w.at[:, chans:c2, 0:chans], w_sem.at[a, 1]),
            pltpu.make_async_copy(from_w.at[:, 0], to_w.at[:, chans:c2, chans:c2], w_sem.at[a, 2]),
        ])
    spans_load = pltpu.make_async_copy(spans_hbm, spans, spans_sem)
    row_load = pltpu.make_async_copy(x_hbm.at[:, rows - 1], rb, row_sem)
    row_load.start()
    for a in range(3):
        for copy in w_loads[a]:
            copy.start()
    spans_load.start()
    for f in order:
        loads[f].start()

    for ref in (p_scale, c_scale, z_scale, from_tm):
        ref[...] = jnp.zeros_like(ref)

    barrier = pltpu.get_barrier_semaphore()
    met = jnp.int32(n_tile - 1)
    for k in around:
        pl.semaphore_signal(barrier, inc=1, device_id=at_tile(k), device_id_type=MESH)
    for k in reach:
        greet(has_tm(k), at_tm(k))
        met = met + has_tm(k).astype(jnp.int32)
    for k in (-1, 1):
        greet(has_both(k), aslant(k))
        met = met + has_both(k).astype(jnp.int32)

    spans_load.wait()
    ends, total = [], jnp.int32(0)
    for c in range(spans.shape[0]):
        total = total + spans[c]
        ends.append(total)
    lows, highs = [], []
    for m in range(CH_DEV):
        slot = tm * CH_DEV + m
        lo, hi = jnp.int32(0), jnp.int32(n_tm * CH_DEV)
        for end in ends:
            lo = jnp.maximum(lo, jnp.where(end <= slot, end, 0))
            hi = jnp.minimum(hi, jnp.where(end > slot, end, n_tm * CH_DEV))
        lows.append(lo)
        highs.append(hi)
    opens = [(lows[m] == tm * CH_DEV + m) for m in range(CH_DEV)]

    wt[:, 0:chans, chans:c2] = jnp.zeros((wt.shape[0], chans, chans), bf16)
    for f in range(xo.shape[0]):
        xo[f, 0] = jnp.zeros((cols, c2), bf16)

    def pair_columns(raw, f):
        for r in range(rows):
            pair = raw(r).reshape(cols, c2)
            if r % 2:
                xo[f, 1 + r // 2] = pair
            else:
                xe[f, r // 2] = pair

    def joined(both):
        moved = pltpu.roll(both[:, chans:c2], 1, 0)
        column = lax.broadcasted_iota(jnp.int32, moved.shape, 0) % cols
        return both[:, 0:chans] + jnp.where(column == 0, 0.0, moved)

    def taps(pairs, into, add=False):
        step = half // 2
        for part in range(2):
            first = part * step
            sums = None
            for a, f in pairs:
                for b, lhs in ((0, xo[f, first : first + step]), (1, xe[f, first : first + step]),
                               (2, xo[f, first + 1 : first + 1 + step])):
                    one = jnp.dot(lhs.reshape(step * cols, c2), wt[3 * a + b], preferred_element_type=f32)
                    sums = one if sums is None else sums + one
            there = slice(first * cols, (first + step) * cols)
            into[there] = into[there] + joined(sums) if add else joined(sums)

    def encode(value, codes, there, most, r):
        top = jnp.maximum(jnp.max(jnp.abs(value), axis=0, keepdims=True), TINY)
        most[r : r + 1] = top
        codes[there] = jnp.round(value * (CODES / top)).astype(jnp.int32).astype(jnp.int16)

    def decode(codes, there, most, r):
        return codes[there].astype(jnp.int32).astype(f32) * (most[r : r + 1] * (1.0 / CODES))

    def row_of(r):
        return slice(r * cols, (r + 1) * cols)

    def ready(f):
        loads[f].wait()
        pair_columns(lambda r: xb[f, r], f)

    def w_ready(a):
        for copy in w_loads[a]:
            copy.wait()

    row_load.wait()
    for f in range(xb.shape[0]):
        ro[f] = rb[f].reshape(cols, c2)
    earlier = [jnp.where(opens[1], ro[4], ro[f]) for f in (2, 3)]
    for a in range(3):
        for copy in w_loads[a]:
            copy.wait()
    by_tap = [
        jnp.dot(jnp.concatenate(stack, axis=0), wt[3 * a], preferred_element_type=f32)
        for a, stack in enumerate((
            [ro[0], earlier[0], ro[4], ro[0], ro[6]],
            [ro[1], earlier[1], ro[5], ro[0], ro[7]],
            [ro[2], ro[4], ro[6], ro[0]],
        ))
    ]
    first_two = by_tap[0] + by_tap[1]
    whole = joined(first_two[0 : 3 * cols] + by_tap[2][0 : 3 * cols])
    own, aside = joined(first_two[3 * cols : 4 * cols]), joined(first_two[4 * cols : 5 * cols])
    z_most[...] = jnp.zeros_like(z_most)
    c_most[...] = jnp.zeros_like(c_most)
    encode(joined(by_tap[2][3 * cols : 4 * cols]) + jnp.where(opens[0], own, 0.0), z_send, row_of(0), z_most, 0)
    for k in (1, 2, 3):
        encode(whole[row_of(k - 1)], z_send, row_of(k), z_most, k)
    encode(aside, c_send, row_of(0), c_most, 0)

    ready(6)
    taps(((0, 6),), p_raw)
    ready(7)
    taps(((1, 7),), p_raw, add=True)
    for r in range(half):
        encode(p_raw[row_of(r)], p_send, row_of(r), p_most, r)
    size = m_rows // 2
    halves = [pl.ds(i * size, size) for i in range(2)]
    above_on, last_on, corner_on = ((has_tile(1), has_tile(-1)), (has_tm(1), has_tm(-1)), (has_both(1), has_both(-1)))
    sent = [
        (z_most, z_scale, at_tile(1), above_on), (z_send, z_recv, at_tile(1), above_on),
        (p_most, p_scale, at_tm(1), last_on), (p_send.at[halves[0]], p_recv.at[halves[0]], at_tm(1), last_on),
        (p_send.at[halves[1]], p_recv.at[halves[1]], at_tm(1), last_on),
        (c_most, c_scale, aslant(1), corner_on), (c_send, c_recv, aslant(1), corner_on),
    ]
    halo = [
        (remote(src, dst, halo_send.at[i], halo_recv.at[i], to), *on) for i, (src, dst, to, on) in enumerate(sent)
    ]
    pl.semaphore_wait(barrier, met)
    for copy, out_on, _ in halo:
        start(copy, out_on)

    ready(0)
    ready(4)
    ready(5)
    taps(((2, 0),), y.at[0])
    taps(((0, 0),), p_own)
    taps(((0, 4), (1, 5), (2, 6)), y.at[3])

    ready(2)
    loads[3].wait()
    pair_columns(lambda r: jnp.where(opens[1], xb[4, r], xb[3, r]), 3)
    pair_columns(lambda r: jnp.where(opens[1], xb[4, r], xb[2, r]), 8)
    ready(1)
    taps(((0, 8), (1, 3), (2, 4)), y.at[2])
    y[1] = p_own[...]
    taps(((1, 1), (2, 2)), y.at[1], add=True)

    def finish(k):
        above = decode(z_recv, row_of(k), z_scale, k)
        if k == 0:
            for copy, _, in_on in halo[2:]:
                wait_recv(copy, in_on)
            above = above + jnp.where(opens[0], 0.0, decode(c_recv, row_of(0), c_scale, 0))
            for r in range(half):
                there = row_of(r)
                y[0, there] = y[0, there] + jnp.where(opens[0], p_own[there], decode(p_recv, there, p_scale, r))
        y[k, 0:cols] = y[k, 0:cols] + jnp.where(tile == 0, 0.0, above)
        mean = jnp.sum(y[k], axis=0, keepdims=True) * (1.0 / m_rows)
        off = y[k] - mean
        return mean, jnp.sum(off * off, axis=0, keepdims=True)

    def pool(means, squares, count):
        mean = functools.reduce(jnp.add, means) * (1.0 / len(means))
        apart = functools.reduce(jnp.add, [(m - mean) * (m - mean) for m in means])
        return mean, functools.reduce(jnp.add, squares) + count * apart

    part = [None] * 4
    for copy, _, in_on in halo[:2]:
        wait_recv(copy, in_on)
    part[3] = finish(3)
    taps(((1, 0),), p_own, add=True)
    for k in (2, 1, 0):
        part[k] = finish(k)
    count = m_rows
    blocks = [pool([part[2 * m][0], part[2 * m + 1][0]], [part[2 * m][1], part[2 * m + 1][1]], count) for m in range(CH_DEV)]
    count *= 2

    fill = jnp.zeros((8 - 2 * CH_DEV, chans), f32)

    def packed(stats):
        return jnp.concatenate([s[0] for s in stats] + [s[1] for s in stats] + [fill], axis=0)

    mine[...] = packed(blocks)
    to_tiles = [
        remote(mine, from_tile.at[k - 1], as_sem.at[k - 1], ar_sem.at[k - 1], at_tile(k)) for k in around
    ]
    for copy in to_tiles:
        copy.start()
    for copy, out_on, _ in halo:
        wait_send(copy, out_on)
    for copy in to_tiles:
        copy.wait_recv()
    all_means = [mine[0:CH_DEV]] + [from_tile[k, 0:CH_DEV] for k in range(n_tile - 1)]
    all_squares = [mine[CH_DEV : 2 * CH_DEV]] + [from_tile[k, CH_DEV : 2 * CH_DEV] for k in range(n_tile - 1)]
    mean, square = pool(all_means, all_squares, count)
    count *= n_tile
    pooled[...] = jnp.concatenate([mean, square, fill], axis=0)

    to_tm = [remote(pooled, from_tm.at[i], bs_sem.at[i], br_sem.at[i], at_tm(k)) for i, k in enumerate(reach)]
    for copy, k in zip(to_tm, reach):
        start(copy, has_tm(k))
    for copy in to_tiles:
        copy.wait_send()
    for copy, k in zip(to_tm, reach):
        wait_recv(copy, has_tm(-k))
    held = [(tm, pooled[...])] + [(tm - k, from_tm[i]) for i, k in enumerate(reach)]

    lane = lax.broadcasted_iota(jnp.int32, (1, chans), 1)

    def over_group(v):
        step = 1
        while step < GROUP:
            v = v + jnp.where((lane // step) % 2 == 1, pltpu.roll(v, step, 1), pltpu.roll(v, chans - step, 1))
            step *= 2
        return v

    rows_out = []
    for m in range(CH_DEV):
        shares = []
        for device, stats in held:
            for q in range(CH_DEV):
                slot = device * CH_DEV + q
                inside = jnp.logical_and(slot >= lows[m], slot < highs[m])
                shares.append((inside, stats[q : q + 1], stats[CH_DEV + q : CH_DEV + q + 1]))
        spans_here = jnp.full((1, chans), (highs[m] - lows[m]).astype(f32))
        clip_mean = functools.reduce(jnp.add, [jnp.where(i, a, 0.0) for i, a, _ in shares]) / spans_here
        mean = over_group(clip_mean) * (1.0 / GROUP)
        spread = functools.reduce(
            jnp.add, [jnp.where(i, s + count * ((a - mean) * (a - mean)), 0.0) for i, a, s in shares]
        )
        variance = over_group(spread) / (spans_here * float(count * GROUP))
        rows_out += [mean, lax.rsqrt(variance + EPS)]
    stat_out[...] = jnp.concatenate(rows_out + [fill], axis=0)

    for copy, k in zip(to_tm, reach):
        wait_send(copy, has_tm(k))


def finishing(y, stats, gain, bias, out_hbm, out, sem):
    copies = []
    for k in range(y.shape[0]):
        m = k // (F // 2)
        normed = (y[k] - stats[2 * m : 2 * m + 1]) * stats[2 * m + 1 : 2 * m + 2] * gain[...] + bias[...]
        halved = 0.5 * normed
        out[k] = (halved * jnp.tanh(halved) + halved).astype(bf16)
        copies.append(pltpu.make_async_copy(out.at[k], out_hbm.at[k], sem.at[k]))
        copies[-1].start()
    for copy in copies:
        copy.wait()


def body(input_frames, clip_spans, conv_weight, norm_gain, norm_bias):
    frames, rows, width, chans = input_frames.shape
    n_tm, n_tile = lax.axis_size("tm"), lax.axis_size("tile")
    half, cols = rows // 2, width // 2
    m_rows = half * cols
    outs = CH_DEV * (F // 2)
    weights = conv_weight.reshape(9, 3, chans, chans)
    n_reach = 2 * REACH
    dma = pltpu.SemaphoreType.DMA
    any_space, vmem = pl.BlockSpec(memory_space=pl.ANY), pl.BlockSpec(memory_space=pltpu.VMEM)
    y, stats = pl.pallas_call(
        functools.partial(kernel, n_tm, n_tile, rows, cols, chans),
        out_shape=[pltpu.VMEM((outs, m_rows, chans), f32), pltpu.VMEM((8, chans), f32)],
        in_specs=[any_space] * 3,
        out_specs=[vmem, vmem],
        scratch_shapes=[
            pltpu.SMEM(clip_spans.shape, jnp.int32),
            pltpu.VMEM((frames, width, chans), bf16),
            pltpu.VMEM((frames, cols, 2 * chans), bf16),
            pltpu.VMEM((frames, rows, width, chans), bf16),
            pltpu.VMEM((frames + 1, half, cols, 2 * chans), bf16),
            pltpu.VMEM((frames + 1, half + 1, cols, 2 * chans), bf16),
            pltpu.VMEM((9, 2 * chans, 2 * chans), bf16),
            pltpu.VMEM((m_rows, chans), f32),
            pltpu.VMEM((m_rows, chans), f32),
            *[
                pltpu.VMEM((n, chans), kind)
                for _ in range(2)
                for n, kind in (
                    (m_rows, jnp.int16), (half, f32), (cols, jnp.int16), (8, f32), (outs * cols, jnp.int16), (8, f32)
                )
            ],
            pltpu.VMEM((8, chans), f32),
            pltpu.VMEM((n_tile - 1, 8, chans), f32),
            pltpu.VMEM((8, chans), f32),
            pltpu.VMEM((n_reach, 8, chans), f32),
            dma, dma, dma((frames,)), dma((3, 3)), dma((7,)), dma((7,)),
            dma((n_tile - 1,)), dma((n_tile - 1,)), dma((n_reach,)), dma((n_reach,)),
        ],
        compiler_params=pltpu.CompilerParams(
            collective_id=0, has_side_effects=True, vmem_limit_bytes=48 * 2**20
        ),
    )(
        pltpu.with_memory_space_constraint(clip_spans, pltpu.HBM),
        input_frames,
        pltpu.with_memory_space_constraint(weights, pltpu.HBM),
    )
    out = pl.pallas_call(
        finishing,
        out_shape=jax.ShapeDtypeStruct((outs, m_rows, chans), bf16),
        in_specs=[vmem] * 4,
        out_specs=any_space,
        scratch_shapes=[pltpu.VMEM((outs, m_rows, chans), bf16), dma((outs,))],
        compiler_params=pltpu.CompilerParams(vmem_limit_bytes=16 * 2**20),
    )(
        pltpu.with_memory_space_constraint(y, pltpu.VMEM),
        pltpu.with_memory_space_constraint(stats, pltpu.VMEM),
        norm_gain.reshape(1, chans),
        norm_bias.reshape(1, chans),
    )
    return out.reshape(outs, half, cols, chans)


def solution(mesh):
    in_specs = (P("tm", "tile", None, None), P(), P(), P(), P())
    out_specs = P("tm", "tile", None, None)
    return jax.shard_map(body, mesh=mesh, in_specs=in_specs, out_specs=out_specs, check_vma=False)
```

```python
import functools

import jax
import jax.numpy as jnp
from jax import lax
from jax.experimental import pallas as pl
from jax.experimental.pallas import tpu as pltpu
from jax.sharding import PartitionSpec as P

F = 4
CH_DEV = 2
GROUP = 4
REACH = 4
EPS = 1e-6
CODES = 32767.0
TINY = 1e-30
PARTS = 2
MESH = pl.DeviceIdType.MESH
f32, bf16 = jnp.float32, jnp.bfloat16


def kernel(
    n_tm, n_tile, rows, cols, chans,
    spans_hbm, x_hbm, w_hbm, y, stat_out,
    spans, rb, ro, xb, xe, xo, wt, p_own, p_raw, p_send, p_most, c_send, c_most, z_send, z_most,
    p_recv, p_scale, c_recv, c_scale, z_recv, z_scale,
    mine, from_tile, pooled, from_tm,
    spans_sem, row_sem, in_sem, w_sem, halo_send, halo_recv, as_sem, ar_sem, bs_sem, br_sem,
):
    tm, tile = lax.axis_index("tm"), lax.axis_index("tile")
    half, c2 = rows // 2, 2 * chans
    m_rows = half * cols
    reach = [sign * k for k in range(REACH, 0, -1) for sign in (-1, 1)]
    around = sorted(range(1, n_tile), key=lambda k: -min(k, n_tile - k))

    def at_tm(k):
        return {"tm": lax.rem(tm + k + n_tm, n_tm)}

    def at_tile(k):
        return {"tile": lax.rem(tile + k + n_tile, n_tile)}

    def aslant(k):
        return at_tm(k) | at_tile(k)

    def has_tm(k):
        return jnp.logical_and(tm + k >= 0, tm + k < n_tm)

    def has_tile(k):
        return jnp.logical_and(tile + k >= 0, tile + k < n_tile)

    def has_both(k):
        return jnp.logical_and(has_tm(k), has_tile(k))

    def greet(there, to):
        @pl.when(there)
        def _():
            pl.semaphore_signal(barrier, inc=1, device_id=to, device_id_type=MESH)

    def start(copy, there):
        @pl.when(there)
        def _():
            copy.start()

    def wait_recv(copy, there):
        @pl.when(there)
        def _():
            copy.wait_recv()

    def wait_send(copy, there):
        @pl.when(there)
        def _():
            copy.wait_send()

    def remote(src, dst, send, recv, where):
        return pltpu.make_async_remote_copy(
            src_ref=src, dst_ref=dst, send_sem=send, recv_sem=recv, device_id=where, device_id_type=MESH
        )

    order = (6, 7, 0, 4, 5, 2, 3, 1)
    loads = {f: pltpu.make_async_copy(x_hbm.at[f], xb.at[f], in_sem.at[f]) for f in order}
    w_loads = []
    for a in range(3):
        from_w, to_w = w_hbm.at[3 * a : 3 * a + 3], wt.at[3 * a : 3 * a + 3]
        w_loads.append([
            pltpu.make_async_copy(from_w.at[:, 1], to_w.at[:, 0:chans, 0:chans], w_sem.at[a, 0]),
            pltpu.make_async_copy(from_w.at[:, 2], to_w.at[:, chans:c2, 0:chans], w_sem.at[a, 1]),
            pltpu.make_async_copy(from_w.at[:, 0], to_w.at[:, chans:c2, chans:c2], w_sem.at[a, 2]),
        ])
    spans_load = pltpu.make_async_copy(spans_hbm, spans, spans_sem)
    row_load = pltpu.make_async_copy(x_hbm.at[:, rows - 1], rb, row_sem)
    row_load.start()
    for a in range(3):
        for copy in w_loads[a]:
            copy.start()
    spans_load.start()
    for f in order:
        loads[f].start()

    for ref in (p_scale, c_scale, z_scale, from_tm):
        ref[...] = jnp.zeros_like(ref)

    barrier = pltpu.get_barrier_semaphore()
    met = jnp.int32(n_tile - 1)
    for k in around:
        pl.semaphore_signal(barrier, inc=1, device_id=at_tile(k), device_id_type=MESH)
    for k in reach:
        greet(has_tm(k), at_tm(k))
        met = met + has_tm(k).astype(jnp.int32)
    for k in (-1, 1):
        greet(has_both(k), aslant(k))
        met = met + has_both(k).astype(jnp.int32)

    spans_load.wait()
    ends, total = [], jnp.int32(0)
    for c in range(spans.shape[0]):
        total = total + spans[c]
        ends.append(total)
    lows, highs = [], []
    for m in range(CH_DEV):
        slot = tm * CH_DEV + m
        lo, hi = jnp.int32(0), jnp.int32(n_tm * CH_DEV)
        for end in ends:
            lo = jnp.maximum(lo, jnp.where(end <= slot, end, 0))
            hi = jnp.minimum(hi, jnp.where(end > slot, end, n_tm * CH_DEV))
        lows.append(lo)
        highs.append(hi)
    opens = [(lows[m] == tm * CH_DEV + m) for m in range(CH_DEV)]

    wt[:, 0:chans, chans:c2] = jnp.zeros((wt.shape[0], chans, chans), bf16)
    for f in range(xo.shape[0]):
        xo[f, 0] = jnp.zeros((cols, c2), bf16)

    def pair_columns(raw, f):
        for r in range(rows):
            pair = raw(r).reshape(cols, c2)
            if r % 2:
                xo[f, 1 + r // 2] = pair
            else:
                xe[f, r // 2] = pair

    def joined(both):
        moved = pltpu.roll(both[:, chans:c2], 1, 0)
        column = lax.broadcasted_iota(jnp.int32, moved.shape, 0) % cols
        return both[:, 0:chans] + jnp.where(column == 0, 0.0, moved)

    def taps(pairs, into, add=False):
        step = half // 2
        for part in range(2):
            first = part * step
            sums = None
            for a, f in pairs:
                for b, lhs in ((0, xo[f, first : first + step]), (1, xe[f, first : first + step]),
                               (2, xo[f, first + 1 : first + 1 + step])):
                    one = jnp.dot(lhs.reshape(step * cols, c2), wt[3 * a + b], preferred_element_type=f32)
                    sums = one if sums is None else sums + one
            there = slice(first * cols, (first + step) * cols)
            into[there] = into[there] + joined(sums) if add else joined(sums)

    def encode(value, codes, there, most, r):
        top = jnp.maximum(jnp.max(jnp.abs(value), axis=0, keepdims=True), TINY)
        most[r : r + 1] = top
        codes[there] = jnp.round(value * (CODES / top)).astype(jnp.int32).astype(jnp.int16)

    def decode(codes, there, most, r):
        return codes[there].astype(jnp.int32).astype(f32) * (most[r : r + 1] * (1.0 / CODES))

    def row_of(r):
        return slice(r * cols, (r + 1) * cols)

    def ready(f):
        loads[f].wait()
        pair_columns(lambda r: xb[f, r], f)

    def w_ready(a):
        for copy in w_loads[a]:
            copy.wait()

    row_load.wait()
    for f in range(xb.shape[0]):
        ro[f] = rb[f].reshape(cols, c2)
    earlier = [jnp.where(opens[1], ro[4], ro[f]) for f in (2, 3)]
    for a in range(3):
        for copy in w_loads[a]:
            copy.wait()
    by_tap = [
        jnp.dot(jnp.concatenate(stack, axis=0), wt[3 * a], preferred_element_type=f32)
        for a, stack in enumerate((
            [ro[0], earlier[0], ro[4], ro[0], ro[6]],
            [ro[1], earlier[1], ro[5], ro[0], ro[7]],
            [ro[2], ro[4], ro[6], ro[0]],
        ))
    ]
    first_two = by_tap[0] + by_tap[1]
    whole = joined(first_two[0 : 3 * cols] + by_tap[2][0 : 3 * cols])
    own, aside = joined(first_two[3 * cols : 4 * cols]), joined(first_two[4 * cols : 5 * cols])
    z_most[...] = jnp.zeros_like(z_most)
    c_most[...] = jnp.zeros_like(c_most)
    encode(joined(by_tap[2][3 * cols : 4 * cols]) + jnp.where(opens[0], own, 0.0), z_send, row_of(0), z_most, 0)
    for k in (1, 2, 3):
        encode(whole[row_of(k - 1)], z_send, row_of(k), z_most, k)
    encode(aside, c_send, row_of(0), c_most, 0)

    ready(6)
    taps(((0, 6),), p_raw)
    ready(7)
    taps(((1, 7),), p_raw, add=True)
    for r in range(half):
        encode(p_raw[row_of(r)], p_send, row_of(r), p_most, r)
    size = m_rows // 2
    halves = [pl.ds(i * size, size) for i in range(2)]
    above_on, last_on, corner_on = ((has_tile(1), has_tile(-1)), (has_tm(1), has_tm(-1)), (has_both(1), has_both(-1)))
    sent = [
        (z_most, z_scale, at_tile(1), above_on), (z_send, z_recv, at_tile(1), above_on),
        (p_most, p_scale, at_tm(1), last_on), (p_send.at[halves[0]], p_recv.at[halves[0]], at_tm(1), last_on),
        (p_send.at[halves[1]], p_recv.at[halves[1]], at_tm(1), last_on),
        (c_most, c_scale, aslant(1), corner_on), (c_send, c_recv, aslant(1), corner_on),
    ]
    halo = [
        (remote(src, dst, halo_send.at[i], halo_recv.at[i], to), *on) for i, (src, dst, to, on) in enumerate(sent)
    ]
    pl.semaphore_wait(barrier, met)
    for copy, out_on, _ in halo[2:] + halo[:2]:
        start(copy, out_on)

    ready(0)
    ready(4)
    ready(5)
    taps(((2, 0),), y.at[0])
    taps(((0, 0),), p_own)
    taps(((0, 4), (1, 5), (2, 6)), y.at[3])

    ready(2)
    loads[3].wait()
    pair_columns(lambda r: jnp.where(opens[1], xb[4, r], xb[3, r]), 3)
    pair_columns(lambda r: jnp.where(opens[1], xb[4, r], xb[2, r]), 8)
    ready(1)
    taps(((0, 8), (1, 3), (2, 4)), y.at[2])
    y[1] = p_own[...]
    taps(((1, 1), (2, 2)), y.at[1], add=True)

    def finish(k):
        above = decode(z_recv, row_of(k), z_scale, k)
        if k == 0:
            for copy, _, in_on in halo[2:]:
                wait_recv(copy, in_on)
            above = above + jnp.where(opens[0], 0.0, decode(c_recv, row_of(0), c_scale, 0))
            for r in range(half):
                there = row_of(r)
                y[0, there] = y[0, there] + jnp.where(opens[0], p_own[there], decode(p_recv, there, p_scale, r))
        y[k, 0:cols] = y[k, 0:cols] + jnp.where(tile == 0, 0.0, above)
        mean = jnp.sum(y[k], axis=0, keepdims=True) * (1.0 / m_rows)
        off = y[k] - mean
        return mean, jnp.sum(off * off, axis=0, keepdims=True)

    def pool(means, squares, count):
        mean = functools.reduce(jnp.add, means) * (1.0 / len(means))
        apart = functools.reduce(jnp.add, [(m - mean) * (m - mean) for m in means])
        return mean, functools.reduce(jnp.add, squares) + count * apart

    part = [None] * 4
    for copy, _, in_on in halo[:2]:
        wait_recv(copy, in_on)
    part[3] = finish(3)
    taps(((1, 0),), p_own, add=True)
    for k in (2, 1, 0):
        part[k] = finish(k)
    count = m_rows
    blocks = [pool([part[2 * m][0], part[2 * m + 1][0]], [part[2 * m][1], part[2 * m + 1][1]], count) for m in range(CH_DEV)]
    count *= 2

    fill = jnp.zeros((8 - 2 * CH_DEV, chans), f32)

    def packed(stats):
        return jnp.concatenate([s[0] for s in stats] + [s[1] for s in stats] + [fill], axis=0)

    mine[...] = packed(blocks)
    to_tiles = [
        remote(mine, from_tile.at[k - 1], as_sem.at[k - 1], ar_sem.at[k - 1], at_tile(k)) for k in around
    ]
    for copy in to_tiles:
        copy.start()
    for copy, out_on, _ in halo:
        wait_send(copy, out_on)
    for copy in to_tiles:
        copy.wait_recv()
    all_means = [mine[0:CH_DEV]] + [from_tile[k, 0:CH_DEV] for k in range(n_tile - 1)]
    all_squares = [mine[CH_DEV : 2 * CH_DEV]] + [from_tile[k, CH_DEV : 2 * CH_DEV] for k in range(n_tile - 1)]
    mean, square = pool(all_means, all_squares, count)
    count *= n_tile
    pooled[...] = jnp.concatenate([mean, square, fill], axis=0)

    to_tm = [remote(pooled, from_tm.at[i], bs_sem.at[i], br_sem.at[i], at_tm(k)) for i, k in enumerate(reach)]
    for copy, k in zip(to_tm, reach):
        start(copy, has_tm(k))
    for copy in to_tiles:
        copy.wait_send()
    for copy, k in zip(to_tm, reach):
        wait_recv(copy, has_tm(-k))
    held = [(tm, pooled[...])] + [(tm - k, from_tm[i]) for i, k in enumerate(reach)]

    lane = lax.broadcasted_iota(jnp.int32, (1, chans), 1)

    def over_group(v):
        step = 1
        while step < GROUP:
            v = v + jnp.where((lane // step) % 2 == 1, pltpu.roll(v, step, 1), pltpu.roll(v, chans - step, 1))
            step *= 2
        return v

    rows_out = []
    for m in range(CH_DEV):
        shares = []
        for device, stats in held:
            for q in range(CH_DEV):
                slot = device * CH_DEV + q
                inside = jnp.logical_and(slot >= lows[m], slot < highs[m])
                shares.append((inside, stats[q : q + 1], stats[CH_DEV + q : CH_DEV + q + 1]))
        spans_here = jnp.full((1, chans), (highs[m] - lows[m]).astype(f32))
        clip_mean = functools.reduce(jnp.add, [jnp.where(i, a, 0.0) for i, a, _ in shares]) / spans_here
        mean = over_group(clip_mean) * (1.0 / GROUP)
        spread = functools.reduce(
            jnp.add, [jnp.where(i, s + count * ((a - mean) * (a - mean)), 0.0) for i, a, s in shares]
        )
        variance = over_group(spread) / (spans_here * float(count * GROUP))
        rows_out += [mean, lax.rsqrt(variance + EPS)]
    stat_out[...] = jnp.concatenate(rows_out + [fill], axis=0)

    for copy, k in zip(to_tm, reach):
        wait_send(copy, has_tm(k))


def finishing(y, stats, gain, bias, out_hbm, out, sem):
    copies = []
    part = y.shape[1] // PARTS
    for i in range(y.shape[0] * PARTS):
        k, rows = i // PARTS, pl.ds(i % PARTS * part, part)
        m = k // (F // 2)
        normed = (y[k, rows] - stats[2 * m : 2 * m + 1]) * stats[2 * m + 1 : 2 * m + 2] * gain[...] + bias[...]
        halved = 0.5 * normed
        out[k, rows] = (halved * jnp.tanh(halved) + halved).astype(bf16)
        copies.append(pltpu.make_async_copy(out.at[k, rows], out_hbm.at[k, rows], sem.at[i]))
        copies[-1].start()
    for copy in copies:
        copy.wait()


def body(input_frames, clip_spans, conv_weight, norm_gain, norm_bias):
    frames, rows, width, chans = input_frames.shape
    n_tm, n_tile = lax.axis_size("tm"), lax.axis_size("tile")
    half, cols = rows // 2, width // 2
    m_rows = half * cols
    outs = CH_DEV * (F // 2)
    weights = conv_weight.reshape(9, 3, chans, chans)
    n_reach = 2 * REACH
    dma = pltpu.SemaphoreType.DMA
    any_space, vmem = pl.BlockSpec(memory_space=pl.ANY), pl.BlockSpec(memory_space=pltpu.VMEM)
    y, stats = pl.pallas_call(
        functools.partial(kernel, n_tm, n_tile, rows, cols, chans),
        out_shape=[pltpu.VMEM((outs, m_rows, chans), f32), pltpu.VMEM((8, chans), f32)],
        in_specs=[any_space] * 3,
        out_specs=[vmem, vmem],
        scratch_shapes=[
            pltpu.SMEM(clip_spans.shape, jnp.int32),
            pltpu.VMEM((frames, width, chans), bf16),
            pltpu.VMEM((frames, cols, 2 * chans), bf16),
            pltpu.VMEM((frames, rows, width, chans), bf16),
            pltpu.VMEM((frames + 1, half, cols, 2 * chans), bf16),
            pltpu.VMEM((frames + 1, half + 1, cols, 2 * chans), bf16),
            pltpu.VMEM((9, 2 * chans, 2 * chans), bf16),
            pltpu.VMEM((m_rows, chans), f32),
            pltpu.VMEM((m_rows, chans), f32),
            *[
                pltpu.VMEM((n, chans), kind)
                for _ in range(2)
                for n, kind in (
                    (m_rows, jnp.int16), (half, f32), (cols, jnp.int16), (8, f32), (outs * cols, jnp.int16), (8, f32)
                )
            ],
            pltpu.VMEM((8, chans), f32),
            pltpu.VMEM((n_tile - 1, 8, chans), f32),
            pltpu.VMEM((8, chans), f32),
            pltpu.VMEM((n_reach, 8, chans), f32),
            dma, dma, dma((frames,)), dma((3, 3)), dma((7,)), dma((7,)),
            dma((n_tile - 1,)), dma((n_tile - 1,)), dma((n_reach,)), dma((n_reach,)),
        ],
        compiler_params=pltpu.CompilerParams(
            collective_id=0, has_side_effects=True, vmem_limit_bytes=48 * 2**20
        ),
    )(
        pltpu.with_memory_space_constraint(clip_spans, pltpu.HBM),
        input_frames,
        pltpu.with_memory_space_constraint(weights, pltpu.HBM),
    )
    out = pl.pallas_call(
        finishing,
        out_shape=jax.ShapeDtypeStruct((outs, m_rows, chans), bf16),
        in_specs=[vmem] * 4,
        out_specs=any_space,
        scratch_shapes=[pltpu.VMEM((outs, m_rows, chans), bf16), dma((outs * PARTS,))],
        compiler_params=pltpu.CompilerParams(vmem_limit_bytes=16 * 2**20),
    )(
        pltpu.with_memory_space_constraint(y, pltpu.VMEM),
        pltpu.with_memory_space_constraint(stats, pltpu.VMEM),
        norm_gain.reshape(1, chans),
        norm_bias.reshape(1, chans),
    )
    return out.reshape(outs, half, cols, chans)


def solution(mesh):
    in_specs = (P("tm", "tile", None, None), P(), P(), P(), P())
    out_specs = P("tm", "tile", None, None)
    return jax.shard_map(body, mesh=mesh, in_specs=in_specs, out_specs=out_specs, check_vma=False)
```
